32 devices in a mesh: grp: 2 (over x), gz: 16 (over z, y, core).
Axes of the slice: x: 2, y: 2, z: 4, core: 2. Of those that a mesh axis runs over, the one named last changes fastest.
Arguments:
- features: bfloat16 [12, 128, 32, 128], P(None, ('grp', 'gz')), parts along dimension 1, may hold values from -6 to 6
- w_first: bfloat16 [48, 324], replicated, may hold values from -0.5 to 0.5
- w_second: bfloat16 [96, 1296], replicated, may hold values from -0.25 to 0.25
- w_lift: bfloat16 [48, 96], replicated, may hold values from -0.875 to 0.875
- w_merge: bfloat16 [12, 1296], replicated, may hold values from -0.15625 to 0.15625
- w_affine: bfloat16 [3, 12], replicated, may hold values from -2.5 to 2.5
- tissue: int32 [32, 32], P(('grp', 'gz')), parts along dimension 0, may hold values from 0 to 31, as said below
- owners: int32 [32, 32], P(('grp', 'gz')), parts along dimension 0, may hold values from 0 to 15, as said below
Outputs:
- routed: bfloat16 [32, 16, 2, 1536], P(('grp', 'gz')), parts along dimension 0
The draws below stay inside these ranges and needn't reach their ends.
There are 2 independent parts, one for each index of `grp`. The reference program is written for one: setup_inputs(seed, part) draws one part's arguments, and reference() takes and returns one part's arrays. A program takes and returns all parts, laid end to end along the dimension named above; an argument that names none is the same for every part. Nothing has to cross between parts.
Inputs may be any that keep to these rules, and one draw needn't show every extreme that they name: `tissue`: each row lists 32 different blocks of that device, numbered as in the reference program. `owners`: A device sends at most 2 of its listed blocks to one owner; in every draw some owner receives exactly 2 from every device.
All inputs are finite; a program needn't handle non-finite values.
Results may differ from the reference program's by a relative error of at most 0.0054.
Values may be sent and summed in bfloat16 or wider, within the bound.
A program may use at most 128 MiB of HBM per device.

```python
import jax
import jax.numpy as jnp
from jax import lax

C0 = 12
C1 = 48
C2 = 96
CU = 12
AFF = 3
ZD = 4
NY = 32
NX = 128
BY = 8
BX = 16
TISSUE = 32
SEND_CAP = 2
SLOTS = 32
NZ = 64
NB = 32
TILE = 1536
N_GZ = 16


def draw_tissue(key, part):

    def one_row(source):
        return jax.random.permutation(jax.random.fold_in(key, source), NB)[:TISSUE].astype(jnp.int32)
    return jax.vmap(one_row)(jnp.arange(N_GZ))


def draw_owners(key, part):
    hottest = jax.random.randint(jax.random.fold_in(key, 11), (), 0, N_GZ)
    others = (hottest + 1 + jnp.arange(N_GZ - 1)) % N_GZ
    stocked = jnp.tile(others, SEND_CAP).astype(jnp.int32)

    def one_row(source):
        row_key = jax.random.fold_in(jax.random.fold_in(key, 23), source)
        rest = jax.random.permutation(row_key, stocked)[:TISSUE - SEND_CAP]
        whole = jnp.concatenate([jnp.full((SEND_CAP,), hottest, jnp.int32), rest.astype(jnp.int32)])
        return jax.random.permutation(jax.random.fold_in(row_key, 7), whole).astype(jnp.int32)
    return jax.vmap(one_row)(jnp.arange(N_GZ))


def levels(own_key, shape, pieces, low, high):
    factor_of, own = 1.0, jax.random.fold_in(own_key, 6)
    for dim, parts in pieces:
        draws = jnp.exp(jax.random.uniform(jax.random.fold_in(own, dim), (parts,), jnp.float32, low / len(pieces), high / len(pieces)))
        factor_of = factor_of * jnp.repeat(draws, shape[dim] // parts).reshape([-1 if axis == dim else 1 for axis in range(len(shape))])
    return factor_of


def scatter_about(key, dims, width, most, cuts=(), held_as=jnp.bfloat16):
    loudness = levels(key, dims, cuts, -0.22, 0.18) if cuts else 1.0
    entries = jax.random.normal(key, dims, jnp.float32) * width * loudness
    return jnp.minimum(jnp.maximum(entries, -most), most).astype(held_as)


def setup_inputs(seed: int = 0, part: int = 0) -> dict:
    key_list = jax.random.split(jax.random.key(seed), 9)
    part_keys = jax.random.split(jax.random.fold_in(key_list[8], part), 9)
    features = scatter_about(part_keys[0], (C0, NZ, NY, NX), 1.0, 6.0, ((1, 16),))
    w_first = scatter_about(key_list[1], (C1, 27 * C0), (27 * C0 // 2) ** -0.5, 0.5)
    w_second = scatter_about(key_list[2], (C2, 27 * C1), (27 * C1 // 2) ** -0.5, 0.25)
    w_lift = scatter_about(key_list[3], (C1, C2), (C2 // 2) ** -0.5, 0.875)
    w_merge = scatter_about(key_list[4], (CU, 27 * C1), (27 * C1) ** -0.5, 0.15625)
    w_affine = scatter_about(key_list[5], (AFF, CU), (CU // 2) ** -0.5, 2.5)
    tissue = draw_tissue(jax.random.fold_in(jax.random.fold_in(key_list[8], part), 71), part)
    owners = draw_owners(jax.random.fold_in(jax.random.fold_in(key_list[8], part), 71), part)
    return dict(features=features, w_first=w_first, w_second=w_second, w_lift=w_lift, w_merge=w_merge, w_affine=w_affine, tissue=tissue, owners=owners)


def convolve(volume, weight, depth_pad):
    kernel = weight.reshape(weight.shape[0], 3, 3, 3, volume.shape[0]).transpose(0, 4, 1, 2, 3)
    result = lax.conv_general_dilated(volume[None], kernel, (1, 1, 1), [(depth_pad, depth_pad), (1, 1), (1, 1)], dimension_numbers=("NCDHW", "OIDHW", "NCDHW"), preferred_element_type=jnp.float32)
    return result[0]


def maxpool(volume):
    shape = volume.shape
    return volume.reshape(shape[0], shape[1] // 2, 2, shape[2] // 2, 2, shape[3] // 2, 2).max(axis=(2, 4, 6))


def upsample(volume):
    shape = volume.shape
    spread = jnp.broadcast_to(volume[:, :, None, :, None, :, None], (shape[0], shape[1], 2, shape[2], 2, shape[3], 2))
    return spread.reshape(shape[0], 2 * shape[1], 2 * shape[2], 2 * shape[3])


def reference(features, w_first, w_second, w_lift, w_merge, w_affine, tissue, owners):
    first_map = jax.nn.relu(convolve(features, w_first, 1)).astype(jnp.bfloat16)
    pooled = maxpool(first_map)
    second_map = jax.nn.relu(convolve(pooled, w_second, 1)).astype(jnp.bfloat16)
    lifted = jnp.einsum("oc,czyx->ozyx", w_lift.astype(jnp.float32), second_map.astype(jnp.float32))
    merged = (upsample(lifted) + first_map.astype(jnp.float32)).astype(jnp.bfloat16)
    third_map = jax.nn.relu(convolve(merged, w_merge, 1))
    affinity = jax.nn.sigmoid(jnp.einsum("ac,czyx->azyx", w_affine.astype(jnp.float32), third_map, precision=lax.Precision.HIGHEST)).astype(jnp.bfloat16)
    tiles = affinity.reshape(AFF, N_GZ, ZD, NY // BY, BY, NX // BX, BX).transpose(1, 3, 5, 0, 2, 4, 6).reshape(N_GZ, NB, TILE)
    same_owner = owners[:, :, None] == owners[:, None, :]
    earlier = jnp.arange(TISSUE)[None, :] < jnp.arange(TISSUE)[:, None]
    ranks = jnp.sum(same_owner & earlier[None], axis=2).astype(jnp.int32)
    slot_index = owners * SEND_CAP + ranks
    slot_pick = (slot_index[:, :, None] == jnp.arange(SLOTS, dtype=jnp.int32)[None, None, :]).astype(jnp.float32)
    block_pick = (tissue[:, :, None] == jnp.arange(NB, dtype=jnp.int32)[None, None, :]).astype(jnp.float32)
    select = jnp.einsum("skt,skb->stb", slot_pick, block_pick)
    outgoing = jnp.einsum("stb,sbe->ste", select, tiles.astype(jnp.float32))
    routed = outgoing.reshape(N_GZ, N_GZ, SEND_CAP, TILE).transpose(1, 0, 2, 3)
    return routed.astype(jnp.bfloat16)
```

```python
import functools

import jax
import jax.numpy as jnp
from jax import lax
from jax.experimental import pallas as pl
from jax.experimental.pallas import tpu as pltpu
from jax.sharding import PartitionSpec as P

BY = 8
BX = 16
SEND_CAP = 2
LANES = 128
ROWS = 16
F32 = jnp.float32
BF16 = jnp.bfloat16


def lane_shift(tile, step, lane):
    rolled = pltpu.roll(tile, step % LANES, axis=1)
    keep = lane >= step if step > 0 else lane < LANES + step
    return jnp.where(keep, rolled, 0.0)


def kernel(
    n, ny,
    f_ref, w1_ref, w2_ref, wl_ref, w3_ref, wa_ref, tissue_ref, owners_ref,
    out_ref,
    fhalo, xpad, fmap, pool, mpad, terms, edge, ehalo, tiles, outgoing,
    fsend, frecv, psend, precv, esend, erecv, asend, arecv,
):
    me = lax.axis_index("gz")
    has_left = me > 0
    has_right = me < n - 1
    left = me - 1
    right = me + 1
    cells = ny * LANES
    hy = ny // 2
    hcells = hy * LANES

    barrier = pltpu.get_barrier_semaphore()

    def greet(step, _):
        pl.semaphore_signal(
            barrier, inc=1, device_id={"gz": lax.rem(me + step, n)},
            device_id_type=pl.DeviceIdType.MESH,
        )
        return 0

    lax.fori_loop(1, n, greet, 0)

    def lanes_of(rows):
        return lax.broadcasted_iota(jnp.int32, (rows, LANES), 1)

    xpad[:, 0:LANES] = jnp.zeros((240, LANES), BF16)
    xpad[:, cells + LANES : cells + 2 * LANES] = jnp.zeros((240, LANES), BF16)
    pool[:, 0:LANES] = jnp.zeros((576, LANES), BF16)
    pool[:, hcells + LANES : hcells + 2 * LANES] = jnp.zeros((576, LANES), BF16)
    mpad[:, 0:LANES] = jnp.zeros((192, LANES), BF16)
    mpad[:, cells + LANES : cells + 2 * LANES] = jnp.zeros((192, LANES), BF16)

    def remote(src, dst, send, recv, target):
        return pltpu.make_async_remote_copy(
            src_ref=src, dst_ref=dst, send_sem=send, recv_sem=recv,
            device_id={"gz": target}, device_id_type=pl.DeviceIdType.MESH,
        )

    def exchange(to_left, at_right, to_right, at_left, send, recv):
        go_left = remote(to_left, at_right, send.at[0], recv.at[0], left)
        go_right = remote(to_right, at_left, send.at[1], recv.at[1], right)

        def start():
            @pl.when(has_left)
            def _():
                go_left.start()

            @pl.when(has_right)
            def _():
                go_right.start()

        def finish():
            @pl.when(has_right)
            def _():
                go_left.wait_recv()

            @pl.when(has_left)
            def _():
                go_right.wait_recv()

            @pl.when(has_left)
            def _():
                go_left.wait_send()

            @pl.when(has_right)
            def _():
                go_right.wait_send()

            @pl.when(jnp.logical_not(has_right))
            def _():
                at_right[...] = jnp.zeros(at_right.shape, at_right.dtype)

            @pl.when(jnp.logical_not(has_left))
            def _():
                at_left[...] = jnp.zeros(at_left.shape, at_left.dtype)

        return start, finish

    pl.semaphore_wait(barrier, n - 1)

    start, finish = exchange(
        f_ref.at[0:16], fhalo.at[16:32], f_ref.at[32:48], fhalo.at[0:16], fsend, frecv
    )
    start()
    finish()

    def shift_features(y, _):
        at = pl.ds(pl.multiple_of(y * LANES, LANES), LANES)
        to = pl.ds(pl.multiple_of((y + 1) * LANES, LANES), LANES)
        lane = lanes_of(80)
        v = jnp.concatenate([fhalo[0:16, at], f_ref[:, at], fhalo[16:32, at]], axis=0)
        vf = v.astype(F32)
        xpad[0:80, to] = lane_shift(vf, 1, lane).astype(BF16)
        xpad[80:160, to] = v
        xpad[160:240, to] = lane_shift(vf, -1, lane).astype(BF16)
        return 0

    lax.fori_loop(0, ny, shift_features, 0, unroll=2)

    def shift_pool(row0, rows, v, to):
        lane = lanes_of(rows)
        pool[row0 : row0 + rows, to] = lane_shift(v, 2, lane).astype(BF16)
        pool[384 + row0 : 384 + row0 + rows, to] = lane_shift(v, -2, lane).astype(BF16)

    def first_conv(i, _):
        base = pl.multiple_of(i * 2 * LANES, 2 * LANES)
        patch = jnp.concatenate(
            [
                xpad[:, pl.ds(pl.multiple_of(base + b * LANES, LANES), 2 * LANES)]
                for b in range(3)
            ],
            axis=0,
        )
        acc = jnp.maximum(jnp.dot(w1_ref[...], patch, preferred_element_type=F32), 0.0)
        fmap[:, pl.ds(base, 2 * LANES)] = acc.astype(BF16)
        deep = jnp.concatenate(
            [jnp.maximum(acc[0:48], acc[48:96]), jnp.maximum(acc[96:144], acc[144:192])], axis=0
        )
        wide = jnp.maximum(deep[:, 0:LANES], deep[:, LANES : 2 * LANES])
        even = lax.rem(lanes_of(96), 2) == 0
        other = jnp.where(
            even, pltpu.roll(wide, LANES - 1, axis=1), pltpu.roll(wide, 1, axis=1)
        )
        both = jnp.maximum(wide, other)
        to = pl.ds(pl.multiple_of((i + 1) * LANES, LANES), LANES)
        pool[240:336, to] = both.astype(BF16)
        shift_pool(48, 96, both, to)
        return 0

    lax.fori_loop(0, hy, first_conv, 0, unroll=2)

    inner = pl.ds(LANES, hcells)
    start, finish = exchange(
        pool.at[240:288, inner], pool.at[336:384, inner],
        pool.at[288:336, inner], pool.at[192:240, inner], psend, precv,
    )
    start()
    finish()

    def shift_halo(y, _):
        to = pl.ds(pl.multiple_of((y + 1) * LANES, LANES), LANES)
        shift_pool(0, 48, pool[192:240, to].astype(F32), to)
        shift_pool(144, 48, pool[336:384, to].astype(F32), to)
        return 0

    lax.fori_loop(0, hy, shift_halo, 0, unroll=2)

    def second_conv(i, _):
        base = pl.multiple_of(i * 2 * LANES, 2 * LANES)
        patch = jnp.concatenate(
            [
                pool[:, pl.ds(pl.multiple_of(base + b * LANES, LANES), 2 * LANES)]
                for b in range(3)
            ],
            axis=0,
        )
        acc = jnp.dot(w2_ref[...], patch, preferred_element_type=F32)
        second = jnp.maximum(acc, 0.0).astype(BF16)
        for half in range(2):
            lifted = jnp.dot(
                wl_ref[...], second[96 * half : 96 * half + 96], preferred_element_type=F32
            )
            for row in range(4):
                part = lifted[:, (row // 2) * LANES : (row // 2 + 1) * LANES]
                for deep in range(2):
                    plane = 48 * (2 * half + deep)
                    own = fmap[
                        plane : plane + 48,
                        pl.ds(pl.multiple_of(i * 4 * LANES + row * LANES, LANES), LANES),
                    ]
                    mpad[
                        plane : plane + 48,
                        pl.ds(pl.multiple_of(i * 4 * LANES + (row + 1) * LANES, LANES), LANES),
                    ] = (part + own.astype(F32)).astype(BF16)
        return 0

    lax.fori_loop(0, hy // 2, second_conv, 0)

    def third_conv(i, _):
        base = pl.multiple_of(i * 2 * LANES, 2 * LANES)
        patch = jnp.concatenate(
            [
                mpad[:, pl.ds(pl.multiple_of(base + b * LANES, LANES), 2 * LANES)]
                for b in range(3)
            ],
            axis=0,
        )
        acc = jnp.dot(w3_ref[...], patch, preferred_element_type=F32)
        lane = lanes_of(72)
        for row in range(2):
            at = slice(row * LANES, (row + 1) * LANES)
            total = (
                acc[72:144, at]
                + lane_shift(acc[0:72, at], 1, lane)
                + lane_shift(acc[144:216, at], -1, lane)
            )
            to = pl.ds(pl.multiple_of(base + row * LANES, LANES), LANES)
            terms[:, to] = total
            edge[0:16, to] = total[0:16].astype(BF16)
            edge[16:32, to] = total[56:72].astype(BF16)
        return 0

    lax.fori_loop(0, hy, third_conv, 0, unroll=2)

    start, finish = exchange(
        edge.at[0:16], ehalo.at[16:32], edge.at[16:32], ehalo.at[0:16], esend, erecv
    )
    start()
    finish()

    spread_row = lax.broadcasted_iota(jnp.int32, (BY * LANES, LANES), 0)
    spread_col = lax.broadcasted_iota(jnp.int32, (BY * LANES, LANES), 1)
    spread = jnp.where(
        spread_col == (spread_row // LANES) * BX + lax.rem(spread_row, BX), 1.0, 0.0
    ).astype(BF16)
    nbx = LANES // BX
    block_mask = (
        lax.broadcasted_iota(jnp.int32, (nbx * ROWS, LANES), 0) // ROWS
        == lax.broadcasted_iota(jnp.int32, (nbx * ROWS, LANES), 1) // BX
    )

    def head(by, _):
        parts = []
        for pair in range(BY // 2):
            at = pl.ds(pl.multiple_of((by * BY + 2 * pair) * LANES, LANES), 2 * LANES)
            total = terms[:, at]
            low = total[8:24] + ehalo[0:16, at].astype(F32)
            high = total[48:64] + ehalo[16:32, at].astype(F32)
            third = jnp.maximum(
                jnp.concatenate([total[0:8], low, total[24:48], high, total[64:72]], axis=0), 0.0
            )
            one = third.astype(BF16).astype(F32)
            rest = third - one
            two = rest.astype(BF16).astype(F32)
            three = rest - two
            split = jnp.concatenate([one, two, three], axis=0).astype(BF16)
            logits = jnp.dot(wa_ref[...], split, preferred_element_type=F32)
            affinity = 1.0 / (1.0 + jnp.exp(-logits))
            for row in range(2):
                tile = affinity[:, row * LANES : (row + 1) * LANES]
                stacked = jnp.concatenate([tile] * nbx, axis=0)
                parts.append(jnp.where(block_mask, stacked, 0.0).astype(BF16))
        spread_out = jnp.concatenate(parts, axis=1)
        rows = nbx * ROWS
        tiles[pl.ds(pl.multiple_of(by * rows, rows), rows), :] = jnp.dot(
            spread_out, spread, preferred_element_type=F32
        ).astype(BF16)
        return 0

    lax.fori_loop(0, ny // BY, head, 0)

    count = tissue_ref.shape[1]
    blocks = (ny // BY) * nbx
    shape = (count, count)
    r = lax.broadcasted_iota(jnp.int32, shape, 0)
    c = lax.broadcasted_iota(jnp.int32, shape, 1)
    own_row = jnp.broadcast_to(owners_ref[...], shape)
    tis_row = jnp.broadcast_to(tissue_ref[...], shape)
    own_col = jnp.sum(jnp.where(r == c, own_row, 0), axis=1, keepdims=True)
    tis_col = jnp.sum(jnp.where(r == c, tis_row, 0), axis=1, keepdims=True)
    rank = jnp.sum(jnp.where((own_row == own_col) & (c < r), 1, 0), axis=1, keepdims=True)
    slot_col = own_col * SEND_CAP + rank
    wide_shape = (count, blocks * ROWS)
    block_of = lax.broadcasted_iota(jnp.int32, wide_shape, 1) // ROWS
    slot_row = (
        jnp.sum(jnp.where(tis_col == block_of, slot_col + 1, 0), axis=0, keepdims=True) - 1
    )

    group = 256

    def route(g, _):
        row = lax.broadcasted_iota(jnp.int32, (group, blocks * ROWS), 0) + g * group
        col = lax.broadcasted_iota(jnp.int32, (group, blocks * ROWS), 1)
        pick = (row // ROWS == slot_row) & (lax.rem(row, ROWS) == lax.rem(col, ROWS))
        pick = jnp.where(pick, 1.0, 0.0).astype(BF16)
        outgoing[pl.ds(pl.multiple_of(g * group, group), group), :] = jnp.dot(
            pick, tiles[...], preferred_element_type=F32
        ).astype(BF16)
        return 0

    lax.fori_loop(0, n * SEND_CAP * ROWS // group, route, 0)

    per = SEND_CAP * ROWS

    def message(step):
        target = lax.rem(me + step, n)
        return remote(
            outgoing.at[pl.ds(pl.multiple_of(target * per, per), per)],
            out_ref.at[me], asend.at[step], arecv.at[step], target,
        )

    def send(step, _):
        message(step).start()
        return 0

    def receive(step, _):
        message(step).wait()
        return 0

    lax.fori_loop(1, n, send, 0)
    out_ref[me] = outgoing[pl.ds(pl.multiple_of(me * per, per), per), :]
    lax.fori_loop(1, n, receive, 0)


def banded_weights(w_first, w_second, w_merge, w_affine, depth):
    c1, c0 = w_first.shape[0], w_first.shape[1] // 27
    c2 = w_second.shape[0]
    cu = w_merge.shape[0]
    zero = jnp.zeros((), BF16)

    def by_offset(w, channels):
        out = w.shape[0]
        return w.reshape(out, 3, 9, channels).transpose(0, 2, 1, 3).reshape(out, 9, 3 * channels)

    one = by_offset(w_first, c0)
    first = jnp.stack(
        [
            lax.pad(one, zero, ((0, 0, 0), (0, 0, 0), (4 + c0 * z, 80 - 4 - c0 * z - 3 * c0, 0)))
            for z in range(depth)
        ]
    ).reshape(depth * c1, 9 * 80)
    two = by_offset(w_second, c1)
    half = depth // 2
    second = jnp.stack(
        [
            lax.pad(two, zero, ((0, 0, 0), (0, 0, 0), (c1 * z, c1 * (half - 1 - z), 0)))
            for z in range(half)
        ]
    ).reshape(half * c2, 9 * (half + 2) * c1)
    three = (
        w_merge.reshape(cu, 3, 3, 3, c1).transpose(3, 0, 2, 1, 4).reshape(3, cu, 3, 3 * c1)
    )
    none = (0, 0, 0)
    third = jnp.stack(
        [
            lax.pad(three, zero, (none, none, none, (c1 * zo - 2 * c1, c1 * (depth + 1 - zo) - 2 * c1, 0)))
            for zo in range(depth + 2)
        ],
        axis=1,
    ).reshape(3 * (depth + 2) * cu, 3 * depth * c1)
    aff = w_affine.shape[0]
    place = jnp.eye(depth, depth + 2, 1, dtype=BF16)
    heads = (w_affine[:, None, None, :] * place[None, :, :, None]).reshape(
        aff * depth, (depth + 2) * cu
    )
    heads = jnp.pad(jnp.concatenate([heads] * 3, axis=1), ((0, ROWS - aff * depth), (0, 0)))
    return first, second, third, heads


def on_device(features, w_first, w_second, w_lift, w_merge, w_affine, tissue, owners):
    n = lax.axis_size("gz")
    channels, depth, ny, nx = features.shape
    cells = ny * nx
    hcells = (ny // 2) * nx
    flat = features.transpose(1, 0, 2, 3).reshape(depth * channels, cells)
    first, second, third, heads = banded_weights(w_first, w_second, w_merge, w_affine, depth)
    per = SEND_CAP * ROWS
    blocks = (ny // BY) * (nx // BX)
    vmem = pl.BlockSpec(memory_space=pltpu.VMEM)
    routed = pl.pallas_call(
        functools.partial(kernel, n, ny),
        out_shape=jax.ShapeDtypeStruct((n, per, LANES), BF16),
        in_specs=[vmem] * 8,
        out_specs=vmem,
        scratch_shapes=[
            pltpu.VMEM((32, cells), BF16),
            pltpu.VMEM((240, cells + 2 * LANES), BF16),
            pltpu.VMEM((192, cells), BF16),
            pltpu.VMEM((576, hcells + 2 * LANES), BF16),
            pltpu.VMEM((192, cells + 2 * LANES), BF16),
            pltpu.VMEM((72, cells), F32),
            pltpu.VMEM((32, cells), BF16),
            pltpu.VMEM((32, cells), BF16),
            pltpu.VMEM((blocks * ROWS, LANES), BF16),
            pltpu.VMEM((n * per, LANES), BF16),
            pltpu.SemaphoreType.DMA((2,)),
            pltpu.SemaphoreType.DMA((2,)),
            pltpu.SemaphoreType.DMA((2,)),
            pltpu.SemaphoreType.DMA((2,)),
            pltpu.SemaphoreType.DMA((2,)),
            pltpu.SemaphoreType.DMA((2,)),
            pltpu.SemaphoreType.DMA((n,)),
            pltpu.SemaphoreType.DMA((n,)),
        ],
        compiler_params=pltpu.CompilerParams(
            collective_id=0, has_side_effects=True, vmem_limit_bytes=48 * 1024 * 1024
        ),
        cost_estimate=pl.CostEstimate(
            flops=1600000000, bytes_accessed=2000000, transcendentals=65536
        ),
    )(flat, first, second, w_lift, third, heads, tissue, owners)
    used = w_affine.shape[0] * depth
    return routed.reshape(n, SEND_CAP, ROWS, LANES)[:, :, :used].reshape(
        1, n, SEND_CAP, used * LANES
    )


def solution(mesh):
    placed = (
        P(None, ("grp", "gz"), None, None),
        P(),
        P(),
        P(),
        P(),
        P(),
        P(("grp", "gz"), None),
        P(("grp", "gz"), None),
    )
    return jax.shard_map(
        on_device,
        mesh=mesh,
        in_specs=placed,
        out_specs=P(("grp", "gz"), None, None, None),
        check_vma=False,
    )
```

```python
import functools

import jax
import jax.numpy as jnp
import ml_dtypes
import numpy as np
from jax import lax
from jax.experimental import pallas as pl
from jax.experimental.pallas import tpu as pltpu
from jax.sharding import PartitionSpec as P

BY = 8
BX = 16
SEND_CAP = 2
LANES = 128
PART = 8
SEGS = 4
F32 = jnp.float32
BF16 = jnp.bfloat16


def lane_shift(tile, step, lane):
    rolled = pltpu.roll(tile, step % LANES, axis=1)
    keep = lane >= step if step > 0 else lane < LANES + step
    return jnp.where(keep, rolled, 0.0)


def kernel(
    n, ny,
    f_ref, w1_ref, w2_ref, wl_ref, w3_ref, wa_ref, tissue_ref, owners_ref,
    out_ref,
    fhalo, xpad, fmap, pool, mpad, terms, edge, ehalo, w2_band, picks, tiles, outgoing,
    fsend, frecv, psend, precv, esend, erecv, asend, arecv,
):
    me = lax.axis_index("gz")
    has_left = me > 0
    has_right = me < n - 1
    left = me - 1
    right = me + 1
    cells = ny * LANES
    hy = ny // 2
    hcells = hy * LANES

    barrier = pltpu.get_barrier_semaphore()

    def greet(step, _):
        pl.semaphore_signal(
            barrier, inc=1, device_id={"gz": lax.rem(me + step, n)},
            device_id_type=pl.DeviceIdType.MESH,
        )
        return 0

    lax.fori_loop(1, n, greet, 0)

    def lanes_of(rows):
        return lax.broadcasted_iota(jnp.int32, (rows, LANES), 1)

    xpad[:, 0:LANES] = jnp.zeros((240, LANES), BF16)
    xpad[:, cells + LANES : cells + 2 * LANES] = jnp.zeros((240, LANES), BF16)
    pool[:, 0:LANES] = jnp.zeros((576, LANES), BF16)
    pool[:, hcells + LANES : hcells + 2 * LANES] = jnp.zeros((576, LANES), BF16)
    mpad[:, 0:LANES] = jnp.zeros((192, LANES), BF16)
    mpad[:, cells + LANES : cells + 2 * LANES] = jnp.zeros((192, LANES), BF16)

    def remote(src, dst, send, recv, target):
        return pltpu.make_async_remote_copy(
            src_ref=src, dst_ref=dst, send_sem=send, recv_sem=recv,
            device_id={"gz": target}, device_id_type=pl.DeviceIdType.MESH,
        )

    def exchange(to_left, at_right, to_right, at_left, send, recv, seg):
        go_left = remote(to_left, at_right, send.at[0, seg], recv.at[0, seg], left)
        go_right = remote(to_right, at_left, send.at[1, seg], recv.at[1, seg], right)

        def start():
            @pl.when(has_left)
            def _():
                go_left.start()

            @pl.when(has_right)
            def _():
                go_right.start()

        def receive():
            @pl.when(has_right)
            def _():
                go_left.wait_recv()

            @pl.when(has_left)
            def _():
                go_right.wait_recv()

            @pl.when(jnp.logical_not(has_right))
            def _():
                at_right[...] = jnp.zeros(at_right.shape, at_right.dtype)

            @pl.when(jnp.logical_not(has_left))
            def _():
                at_left[...] = jnp.zeros(at_left.shape, at_left.dtype)

        def sent():
            @pl.when(has_left)
            def _():
                go_left.wait_send()

            @pl.when(has_right)
            def _():
                go_right.wait_send()

        return start, receive, sent

    pl.semaphore_wait(barrier, n - 1)

    features_start, features_receive, features_sent = exchange(
        f_ref.at[0:16], fhalo.at[16:32], f_ref.at[32:48], fhalo.at[0:16], fsend, frecv, 0
    )
    features_start()

    nbx = LANES // BX
    count = tissue_ref.shape[1]
    blocks = (ny // BY) * nbx
    shape = (count, count)
    r = lax.broadcasted_iota(jnp.int32, shape, 0)
    c = lax.broadcasted_iota(jnp.int32, shape, 1)
    own_row = jnp.broadcast_to(owners_ref[...], shape)
    tis_row = jnp.broadcast_to(tissue_ref[...], shape)
    own_col = jnp.sum(jnp.where(r == c, own_row, 0), axis=1, keepdims=True)
    tis_col = jnp.sum(jnp.where(r == c, tis_row, 0), axis=1, keepdims=True)
    rank = jnp.sum(jnp.where((own_row == own_col) & (c < r), 1, 0), axis=1, keepdims=True)
    slot_col = own_col * SEND_CAP + rank
    wide_shape = (count, blocks * PART)
    block_of = lax.broadcasted_iota(jnp.int32, wide_shape, 1) // PART
    slot_row = (
        jnp.sum(jnp.where(tis_col == block_of, slot_col + 1, 0), axis=0, keepdims=True) - 1
    )
    group = 256

    def pick_rows(g, _):
        row = lax.broadcasted_iota(jnp.int32, (group, blocks * PART), 0) + g * group
        col = lax.broadcasted_iota(jnp.int32, (group, blocks * PART), 1)
        pick = (row // PART == slot_row) & (lax.rem(row, PART) == lax.rem(col, PART))
        picks[pl.ds(pl.multiple_of(g * group, group), group), :] = jnp.where(
            pick, 1.0, 0.0
        ).astype(BF16)
        return 0

    groups = n * SEND_CAP * PART // group
    lax.fori_loop(0, groups, pick_rows, 0)

    w2 = w2_ref[...].astype(F32)
    blank = jnp.zeros((96, 432), F32)
    w2_band[0:96, :] = jnp.concatenate([w2, blank], axis=1).astype(BF16)
    w2_band[96:192, :] = jnp.concatenate([blank, w2], axis=1).astype(BF16)

    features_receive()

    def shift_features(y, _):
        at = pl.ds(pl.multiple_of(y * LANES, LANES), LANES)
        to = pl.ds(pl.multiple_of((y + 1) * LANES, LANES), LANES)
        lane = lanes_of(80)
        v = jnp.concatenate([fhalo[0:16, at], f_ref[:, at], fhalo[16:32, at]], axis=0)
        vf = v.astype(F32)
        xpad[0:80, to] = lane_shift(vf, 1, lane).astype(BF16)
        xpad[80:160, to] = v
        xpad[160:240, to] = lane_shift(vf, -1, lane).astype(BF16)
        return 0

    lax.fori_loop(0, ny, shift_features, 0, unroll=2)

    def shift_pool(row0, rows, v, to):
        lane = lanes_of(rows)
        pool[row0 : row0 + rows, to] = lane_shift(v, 2, lane).astype(BF16)
        pool[384 + row0 : 384 + row0 + rows, to] = lane_shift(v, -2, lane).astype(BF16)

    def first_conv(i, _):
        base = pl.multiple_of(i * 2 * LANES, 2 * LANES)
        patch = jnp.concatenate(
            [
                xpad[:, pl.ds(pl.multiple_of(base + b * LANES, LANES), 2 * LANES)]
                for b in range(3)
            ],
            axis=0,
        )
        acc = jnp.maximum(jnp.dot(w1_ref[...], patch, preferred_element_type=F32), 0.0)
        fmap[:, pl.ds(base, 2 * LANES)] = acc.astype(BF16)
        deep = jnp.concatenate(
            [jnp.maximum(acc[0:48], acc[48:96]), jnp.maximum(acc[96:144], acc[144:192])], axis=0
        )
        wide = jnp.maximum(deep[:, 0:LANES], deep[:, LANES : 2 * LANES])
        even = lax.rem(lanes_of(96), 2) == 0
        other = jnp.where(
            even, pltpu.roll(wide, LANES - 1, axis=1), pltpu.roll(wide, 1, axis=1)
        )
        both = jnp.maximum(wide, other)
        to = pl.ds(pl.multiple_of((i + 1) * LANES, LANES), LANES)
        pool[240:336, to] = both.astype(BF16)
        shift_pool(48, 96, both, to)
        return 0

    seg_rows = hy // SEGS

    def pooled(seg):
        at = pl.ds(pl.multiple_of((seg * seg_rows + 1) * LANES, LANES), seg_rows * LANES)
        return exchange(
            pool.at[240:288, at], pool.at[336:384, at],
            pool.at[288:336, at], pool.at[192:240, at], psend, precv, seg,
        )

    def first_segment(seg, _):
        lax.fori_loop(
            0, seg_rows, lambda i, _: first_conv(seg * seg_rows + i, 0), 0, unroll=2
        )
        pooled(seg)[0]()
        return 0

    lax.fori_loop(0, SEGS, first_segment, 0)

    def shift_halo(y, _):
        to = pl.ds(pl.multiple_of((y + 1) * LANES, LANES), LANES)
        shift_pool(0, 48, pool[192:240, to].astype(F32), to)
        shift_pool(144, 48, pool[336:384, to].astype(F32), to)
        return 0

    def second_conv(i, _):
        base = pl.multiple_of(i * 2 * LANES, 2 * LANES)
        patch = jnp.concatenate(
            [
                pool[
                    192 * c + 48 * plane : 192 * c + 48 * plane + 48,
                    pl.ds(pl.multiple_of(base + b * LANES, LANES), 2 * LANES),
                ]
                for plane in range(4)
                for b in range(3)
                for c in range(3)
            ],
            axis=0,
        )
        acc = jnp.dot(w2_band[...], patch, preferred_element_type=F32)
        second = jnp.maximum(acc, 0.0).astype(BF16)
        for half in range(2):
            lifted = jnp.dot(
                wl_ref[...], second[96 * half : 96 * half + 96], preferred_element_type=F32
            )
            for row in range(4):
                part = lifted[:, (row // 2) * LANES : (row // 2 + 1) * LANES]
                for deep in range(2):
                    plane = 48 * (2 * half + deep)
                    own = fmap[
                        plane : plane + 48,
                        pl.ds(pl.multiple_of(i * 4 * LANES + row * LANES, LANES), LANES),
                    ]
                    mpad[
                        plane : plane + 48,
                        pl.ds(pl.multiple_of(i * 4 * LANES + (row + 1) * LANES, LANES), LANES),
                    ] = (part + own.astype(F32)).astype(BF16)
        return 0

    per_seg = seg_rows // 2
    for seg in range(SEGS):
        pooled(seg)[1]()
        lax.fori_loop(seg * seg_rows, (seg + 1) * seg_rows, shift_halo, 0, unroll=2)
        first = max(seg * per_seg - 1, 0)
        last = (seg + 1) * per_seg - (0 if seg == SEGS - 1 else 1)
        lax.fori_loop(first, last, second_conv, 0)

    def third_conv(i, _):
        base = pl.multiple_of(i * 2 * LANES, 2 * LANES)
        patch = jnp.concatenate(
            [
                mpad[:, pl.ds(pl.multiple_of(base + b * LANES, LANES), 2 * LANES)]
                for b in range(3)
            ],
            axis=0,
        )
        acc = jnp.dot(w3_ref[...], patch, preferred_element_type=F32)
        lane = lanes_of(72)
        for row in range(2):
            at = slice(row * LANES, (row + 1) * LANES)
            total = (
                acc[72:144, at]
                + lane_shift(acc[0:72, at], 1, lane)
                + lane_shift(acc[144:216, at], -1, lane)
            )
            to = pl.ds(pl.multiple_of(base + row * LANES, LANES), LANES)
            terms[:, to] = total
            edge[0:16, to] = total[0:16].astype(BF16)
            edge[16:32, to] = total[56:72].astype(BF16)
        return 0

    def edges(seg):
        at = pl.ds(pl.multiple_of(seg * BY * LANES, BY * LANES), BY * LANES)
        return exchange(
            edge.at[0:16, at], ehalo.at[16:32, at],
            edge.at[16:32, at], ehalo.at[0:16, at], esend, erecv, seg,
        )

    def third_segment(seg, _):
        lax.fori_loop(
            0, BY // 2, lambda i, _: third_conv(seg * (BY // 2) + i, 0), 0, unroll=2
        )
        edges(seg)[0]()
        return 0

    lax.fori_loop(0, ny // BY, third_segment, 0)

    spread_row = lax.broadcasted_iota(jnp.int32, (BY * LANES, LANES), 0)
    spread_col = lax.broadcasted_iota(jnp.int32, (BY * LANES, LANES), 1)
    spread = jnp.where(
        spread_col == (spread_row // LANES) * BX + lax.rem(spread_row, BX), 1.0, 0.0
    ).astype(BF16)
    block_mask = (
        lax.broadcasted_iota(jnp.int32, (nbx * PART, LANES), 0) // PART
        == lax.broadcasted_iota(jnp.int32, (nbx * PART, LANES), 1) // BX
    )
    directions, channels = wa_ref.shape

    def head_matrix(rows, first_at, second_at):
        across = 3 * rows
        inside = lax.rem(lax.broadcasted_iota(jnp.int32, (channels, across), 1), rows)
        channel = lax.broadcasted_iota(jnp.int32, (channels, across), 0)
        hit = (inside == channel + first_at) | (inside == channel + second_at)
        columns = jnp.dot(
            wa_ref[...], jnp.where(hit, 1.0, 0.0).astype(BF16), preferred_element_type=F32
        ).astype(BF16)
        turn = lax.broadcasted_iota(jnp.int32, (PART, directions), 0) // 2
        turn = turn == lax.broadcasted_iota(jnp.int32, (PART, directions), 1)
        full = jnp.dot(
            jnp.where(turn, 1.0, 0.0).astype(BF16), columns, preferred_element_type=F32
        )
        at = lax.rem(lax.broadcasted_iota(jnp.int32, (PART, across), 1), rows)
        odd = lax.rem(lax.broadcasted_iota(jnp.int32, (PART, across), 0), 2) == 1
        start = jnp.where(odd, second_at, first_at)
        keep = (at >= start) & (at < start + channels)
        return jnp.where(keep, full, 0.0).astype(BF16)

    def head_rows(matrix, part, total_of):
        def head(by, _):
            parts = []
            for pair in range(BY // 2):
                at = pl.ds(pl.multiple_of((by * BY + 2 * pair) * LANES, LANES), 2 * LANES)
                third = jnp.maximum(total_of(at), 0.0)
                one = third.astype(BF16).astype(F32)
                rest = third - one
                two = rest.astype(BF16).astype(F32)
                three = rest - two
                split = jnp.concatenate([one, two, three], axis=0).astype(BF16)
                logits = jnp.dot(matrix, split, preferred_element_type=F32)
                affinity = 1.0 / (1.0 + jnp.exp(-logits))
                for row in range(2):
                    tile = affinity[:, row * LANES : (row + 1) * LANES]
                    stacked = jnp.concatenate([tile] * nbx, axis=0)
                    parts.append(jnp.where(block_mask, stacked, 0.0).astype(BF16))
            rows = nbx * PART
            tiles[part, pl.ds(pl.multiple_of(by * rows, rows), rows), :] = jnp.dot(
                jnp.concatenate(parts, axis=1), spread, preferred_element_type=F32
            ).astype(BF16)
            return 0

        return head

    per = SEND_CAP * PART

    def message(part, step):
        target = lax.rem(me + step, n)
        return remote(
            outgoing.at[part, pl.ds(pl.multiple_of(target * per, per), per)],
            out_ref.at[part, me], asend.at[part, step], arecv.at[part, step], target,
        )

    def send_part(part):
        def route(g, _):
            at = pl.ds(pl.multiple_of(g * group, group), group)
            outgoing[part, at, :] = jnp.dot(
                picks[at, :], tiles[part], preferred_element_type=F32
            ).astype(BF16)
            return 0

        def send(step, _):
            message(part, step).start()
            return 0

        lax.fori_loop(0, groups, route, 0)
        lax.fori_loop(1, n, send, 0)
        out_ref[part, me] = outgoing[part, pl.ds(pl.multiple_of(me * per, per), per), :]

    inner_head = head_rows(head_matrix(24, 0, 12), 0, lambda at: terms[24:48, at])
    lax.fori_loop(0, ny // BY, inner_head, 0)
    send_part(0)

    def outer_total(at):
        low = terms[8:24, at] + ehalo[0:16, at].astype(F32)
        high = terms[48:64, at] + ehalo[16:32, at].astype(F32)
        return jnp.concatenate([low, high], axis=0)

    outer_head = head_rows(head_matrix(32, 4, 16), 1, outer_total)

    def outer_segment(by, _):
        edges(by)[1]()
        return outer_head(by, 0)

    lax.fori_loop(0, ny // BY, outer_segment, 0)
    send_part(1)

    features_sent()

    def pooled_sent(seg, _):
        pooled(seg)[2]()
        return 0

    def edges_sent(seg, _):
        edges(seg)[2]()
        return 0

    lax.fori_loop(0, SEGS, pooled_sent, 0)
    lax.fori_loop(0, ny // BY, edges_sent, 0)

    def receive(step, _):
        message(0, step).wait()
        message(1, step).wait()
        return 0

    lax.fori_loop(1, n, receive, 0)


def banded_weights(w_first, w_merge, depth):
    c1, c0 = w_first.shape[0], w_first.shape[1] // 27
    cu = w_merge.shape[0]
    zero = jnp.zeros((), BF16)
    place = np.zeros((depth, 3, 9, c0, 9, 80), np.float32)
    for z in range(depth):
        for a in range(3):
            for i in range(c0):
                for bc in range(9):
                    place[z, a, bc, i, bc, 4 + c0 * (z + a) + i] = 1
    place = place.reshape(depth, 27 * c0, 720).astype(ml_dtypes.bfloat16)
    first = jnp.einsum("oi,zik->zok", w_first, place, preferred_element_type=F32)
    first = first.astype(BF16).reshape(depth * c1, 720)
    three = (
        w_merge.reshape(cu, 3, 3, 3, c1).transpose(3, 0, 2, 1, 4).reshape(3, cu, 3, 3 * c1)
    )
    none = (0, 0, 0)
    third = jnp.stack(
        [
            lax.pad(three, zero, (none, none, none, (c1 * zo - 2 * c1, c1 * (depth + 1 - zo) - 2 * c1, 0)))
            for zo in range(depth + 2)
        ],
        axis=1,
    ).reshape(3 * (depth + 2) * cu, 3 * depth * c1)
    return first, third


def on_device(features, w_first, w_second, w_lift, w_merge, w_affine, tissue, owners):
    n = lax.axis_size("gz")
    channels, depth, ny, nx = features.shape
    cells = ny * nx
    hcells = (ny // 2) * nx
    flat = features.transpose(1, 0, 2, 3).reshape(depth * channels, cells)
    first, third = banded_weights(w_first, w_merge, depth)
    per = SEND_CAP * PART
    blocks = (ny // BY) * (nx // BX)
    vmem = pl.BlockSpec(memory_space=pltpu.VMEM)
    routed = pl.pallas_call(
        functools.partial(kernel, n, ny),
        out_shape=jax.ShapeDtypeStruct((2, n, per, LANES), BF16),
        in_specs=[vmem] * 8,
        out_specs=vmem,
        scratch_shapes=[
            pltpu.VMEM((32, cells), BF16),
            pltpu.VMEM((240, cells + 2 * LANES), BF16),
            pltpu.VMEM((192, cells), BF16),
            pltpu.VMEM((576, hcells + 2 * LANES), BF16),
            pltpu.VMEM((192, cells + 2 * LANES), BF16),
            pltpu.VMEM((72, cells), F32),
            pltpu.VMEM((32, cells), BF16),
            pltpu.VMEM((32, cells), BF16),
            pltpu.VMEM((192, 1728), BF16),
            pltpu.VMEM((n * per, blocks * PART), BF16),
            pltpu.VMEM((2, blocks * PART, LANES), BF16),
            pltpu.VMEM((2, n * per, LANES), BF16),
            pltpu.SemaphoreType.DMA((2, 1)),
            pltpu.SemaphoreType.DMA((2, 1)),
            pltpu.SemaphoreType.DMA((2, SEGS)),
            pltpu.SemaphoreType.DMA((2, SEGS)),
            pltpu.SemaphoreType.DMA((2, ny // BY)),
            pltpu.SemaphoreType.DMA((2, ny // BY)),
            pltpu.SemaphoreType.DMA((2, n)),
            pltpu.SemaphoreType.DMA((2, n)),
        ],
        compiler_params=pltpu.CompilerParams(
            collective_id=0, has_side_effects=True, vmem_limit_bytes=48 * 1024 * 1024
        ),
        cost_estimate=pl.CostEstimate(
            flops=1600000000, bytes_accessed=2000000, transcendentals=65536
        ),
    )(flat, first, w_second, w_lift, third, w_affine, tissue, owners)
    directions = w_affine.shape[0]
    routed = routed.reshape(2, n, SEND_CAP, PART // 2, 2, LANES)[:, :, :, :directions]
    routed = jnp.concatenate(
        [routed[1, :, :, :, :1], routed[0], routed[1, :, :, :, 1:]], axis=3
    )
    return routed.reshape(1, n, SEND_CAP, directions * depth * LANES)


def solution(mesh):
    placed = (
        P(None, ("grp", "gz"), None, None),
        P(),
        P(),
        P(),
        P(),
        P(),
        P(("grp", "gz"), None),
        P(("grp", "gz"), None),
    )
    return jax.shard_map(
        on_device,
        mesh=mesh,
        in_specs=placed,
        out_specs=P(("grp", "gz"), None, None, None),
        check_vma=False,
    )
```

```python
import functools

import jax
import jax.numpy as jnp
import ml_dtypes
import numpy as np
from jax import lax
from jax.experimental import pallas as pl
from jax.experimental.pallas import tpu as pltpu
from jax.sharding import PartitionSpec as P

BY = 8
BX = 16
SEND_CAP = 2
LANES = 128
PART = 8
SEGS = 4
F32 = jnp.float32
BF16 = jnp.bfloat16


def lane_shift(tile, step, lane):
    rolled = pltpu.roll(tile, step % LANES, axis=1)
    keep = lane >= step if step > 0 else lane < LANES + step
    return jnp.where(keep, rolled, 0.0)


def kernel(
    n, ny,
    f_ref, rim_ref, w1_ref, w2_ref, wl_ref, w3_ref, wa_ref, tissue_ref, owners_ref,
    out_ref,
    fhalo, xpad, fmap, pool, mpad, terms, edge, ehalo, w2_band, w3_band, picks, masked, tiles, outgoing,
    fsend, frecv, psend, precv, esend, erecv, asend, arecv,
):
    me = lax.axis_index("gz")
    has_left = me > 0
    has_right = me < n - 1
    left = me - 1
    right = me + 1
    cells = ny * LANES
    hy = ny // 2
    hcells = hy * LANES

    barrier = pltpu.get_barrier_semaphore()

    def greet(step, _):
        pl.semaphore_signal(
            barrier, inc=1, device_id={"gz": lax.rem(me + step, n)},
            device_id_type=pl.DeviceIdType.MESH,
        )
        return 0

    lax.fori_loop(1, n, greet, 0)

    def lanes_of(rows):
        return lax.broadcasted_iota(jnp.int32, (rows, LANES), 1)

    xpad[:, 0:LANES] = jnp.zeros((240, LANES), BF16)
    xpad[:, cells + LANES : cells + 2 * LANES] = jnp.zeros((240, LANES), BF16)
    pool[:, 0:LANES] = jnp.zeros((576, LANES), BF16)
    pool[:, hcells + LANES : hcells + 2 * LANES] = jnp.zeros((576, LANES), BF16)
    mpad[:, 0:LANES] = jnp.zeros((192, LANES), BF16)
    mpad[:, cells + LANES : cells + 2 * LANES] = jnp.zeros((192, LANES), BF16)

    def remote(src, dst, send, recv, target):
        return pltpu.make_async_remote_copy(
            src_ref=src, dst_ref=dst, send_sem=send, recv_sem=recv,
            device_id={"gz": target}, device_id_type=pl.DeviceIdType.MESH,
        )

    def exchange(to_left, at_right, to_right, at_left, send, recv, seg):
        go_left = remote(to_left, at_right, send.at[0, seg], recv.at[0, seg], left)
        go_right = remote(to_right, at_left, send.at[1, seg], recv.at[1, seg], right)

        def start():
            @pl.when(has_left)
            def _():
                go_left.start()

            @pl.when(has_right)
            def _():
                go_right.start()

        def receive():
            @pl.when(has_right)
            def _():
                go_left.wait_recv()

            @pl.when(has_left)
            def _():
                go_right.wait_recv()

            @pl.when(jnp.logical_not(has_right))
            def _():
                at_right[...] = jnp.zeros(at_right.shape, at_right.dtype)

            @pl.when(jnp.logical_not(has_left))
            def _():
                at_left[...] = jnp.zeros(at_left.shape, at_left.dtype)

        def sent():
            @pl.when(has_left)
            def _():
                go_left.wait_send()

            @pl.when(has_right)
            def _():
                go_right.wait_send()

        return start, receive, sent

    pl.semaphore_wait(barrier, n - 1)

    features_start, features_receive, features_sent = exchange(
        rim_ref.at[0:16], fhalo.at[16:32], rim_ref.at[16:32], fhalo.at[0:16], fsend, frecv, 0
    )
    features_start()

    nbx = LANES // BX
    count = tissue_ref.shape[1]
    blocks = (ny // BY) * nbx
    shape = (count, count)
    r = lax.broadcasted_iota(jnp.int32, shape, 0)
    c = lax.broadcasted_iota(jnp.int32, shape, 1)
    own_row = jnp.broadcast_to(owners_ref[...], shape)
    tis_row = jnp.broadcast_to(tissue_ref[...], shape)
    own_col = jnp.sum(jnp.where(r == c, own_row, 0), axis=1, keepdims=True)
    tis_col = jnp.sum(jnp.where(r == c, tis_row, 0), axis=1, keepdims=True)
    rank = jnp.sum(jnp.where((own_row == own_col) & (c < r), 1, 0), axis=1, keepdims=True)
    slot_col = own_col * SEND_CAP + rank
    wide_shape = (count, blocks * PART)
    block_of = lax.broadcasted_iota(jnp.int32, wide_shape, 1) // PART
    slot_row = (
        jnp.sum(jnp.where(tis_col == block_of, slot_col + 1, 0), axis=0, keepdims=True) - 1
    )
    group = 256

    def pick_rows(g, _):
        row = lax.broadcasted_iota(jnp.int32, (group, blocks * PART), 0) + g * group
        col = lax.broadcasted_iota(jnp.int32, (group, blocks * PART), 1)
        pick = (row // PART == slot_row) & (lax.rem(row, PART) == lax.rem(col, PART))
        picks[pl.ds(pl.multiple_of(g * group, group), group), :] = jnp.where(
            pick, 1.0, 0.0
        ).astype(BF16)
        return 0

    groups = n * SEND_CAP * PART // group
    lax.fori_loop(0, groups, pick_rows, 0)

    w2 = w2_ref[...].astype(F32)
    blank = jnp.zeros((96, 432), F32)
    w2_band[0:96, :] = jnp.concatenate([w2, blank], axis=1).astype(BF16)
    w2_band[96:192, :] = jnp.concatenate([blank, w2], axis=1).astype(BF16)

    w3 = w3_ref[...].astype(F32)
    bands = []
    for c_off in range(3):
        columns = jnp.concatenate(
            [w3[:, (3 * ab + c_off) * 48 : (3 * ab + c_off) * 48 + 48] for ab in range(9)], axis=1
        )
        for zo in range(6):
            first = 144 * (zo - 2)
            low, high = max(first, 0), min(first + 432, 576)
            pieces = [columns[:, low - first : high - first]]
            if low > 0:
                pieces.insert(0, jnp.zeros((12, low), F32))
            if high < 576:
                pieces.append(jnp.zeros((12, 576 - high), F32))
            bands.append(jnp.concatenate(pieces, axis=1))
    w3_band[...] = jnp.concatenate(bands, axis=0).astype(BF16)

    def shift_rows(v, row0, to):
        rows = v.shape[0]
        lane = lanes_of(rows)
        vf = v.astype(F32)
        xpad[row0 : row0 + rows, to] = lane_shift(vf, 1, lane).astype(BF16)
        xpad[80 + row0 : 80 + row0 + rows, to] = v
        xpad[160 + row0 : 160 + row0 + rows, to] = lane_shift(vf, -1, lane).astype(BF16)

    def shift_own(y, _):
        at = pl.ds(pl.multiple_of(y * LANES, LANES), LANES)
        to = pl.ds(pl.multiple_of((y + 1) * LANES, LANES), LANES)
        shift_rows(f_ref[:, at], 16, to)
        return 0

    lax.fori_loop(0, ny, shift_own, 0, unroll=4)
    features_receive()

    def shift_rims(y, _):
        at = pl.ds(pl.multiple_of(y * LANES, LANES), LANES)
        to = pl.ds(pl.multiple_of((y + 1) * LANES, LANES), LANES)
        shift_rows(fhalo[0:16, at], 0, to)
        shift_rows(fhalo[16:32, at], 64, to)
        return 0

    lax.fori_loop(0, ny, shift_rims, 0, unroll=4)

    def shift_pool(row0, rows, v, to):
        lane = lanes_of(rows)
        pool[row0 : row0 + rows, to] = lane_shift(v, 2, lane).astype(BF16)
        pool[384 + row0 : 384 + row0 + rows, to] = lane_shift(v, -2, lane).astype(BF16)

    def first_conv(i, _):
        base = pl.multiple_of(i * 2 * LANES, 2 * LANES)
        patch = jnp.concatenate(
            [
                xpad[:, pl.ds(pl.multiple_of(base + b * LANES, LANES), 2 * LANES)]
                for b in range(3)
            ],
            axis=0,
        )
        acc = jnp.maximum(jnp.dot(w1_ref[...], patch, preferred_element_type=F32), 0.0)
        fmap[:, pl.ds(base, 2 * LANES)] = acc.astype(BF16)
        deep = jnp.concatenate(
            [jnp.maximum(acc[0:48], acc[48:96]), jnp.maximum(acc[96:144], acc[144:192])], axis=0
        )
        wide = jnp.maximum(deep[:, 0:LANES], deep[:, LANES : 2 * LANES])
        even = lax.rem(lanes_of(96), 2) == 0
        other = jnp.where(
            even, pltpu.roll(wide, LANES - 1, axis=1), pltpu.roll(wide, 1, axis=1)
        )
        both = jnp.maximum(wide, other)
        to = pl.ds(pl.multiple_of((i + 1) * LANES, LANES), LANES)
        pool[240:336, to] = both.astype(BF16)
        shift_pool(48, 96, both, to)
        return 0

    seg_rows = hy // SEGS

    def pooled(seg):
        at = pl.ds(pl.multiple_of((seg * seg_rows + 1) * LANES, LANES), seg_rows * LANES)
        return exchange(
            pool.at[240:288, at], pool.at[336:384, at],
            pool.at[288:336, at], pool.at[192:240, at], psend, precv, seg,
        )

    def first_segment(seg, _):
        lax.fori_loop(
            0, seg_rows, lambda i, _: first_conv(seg * seg_rows + i, 0), 0, unroll=True
        )
        pooled(seg)[0]()
        return 0

    lax.fori_loop(0, SEGS, first_segment, 0)

    def shift_halo(y, _):
        to = pl.ds(pl.multiple_of((y + 1) * LANES, LANES), LANES)
        shift_pool(0, 48, pool[192:240, to].astype(F32), to)
        shift_pool(144, 48, pool[336:384, to].astype(F32), to)
        return 0

    def second_conv(i, _):
        base = pl.multiple_of(i * 2 * LANES, 2 * LANES)
        patch = jnp.concatenate(
            [
                pool[
                    192 * c + 48 * plane : 192 * c + 48 * plane + 48,
                    pl.ds(pl.multiple_of(base + b * LANES, LANES), 2 * LANES),
                ]
                for plane in range(4)
                for b in range(3)
                for c in range(3)
            ],
            axis=0,
        )
        acc = jnp.dot(w2_band[...], patch, preferred_element_type=F32)
        second = jnp.maximum(acc, 0.0).astype(BF16)
        for half in range(2):
            lifted = jnp.dot(
                wl_ref[...], second[96 * half : 96 * half + 96], preferred_element_type=F32
            )
            for row in range(4):
                part = lifted[:, (row // 2) * LANES : (row // 2 + 1) * LANES]
                for deep in range(2):
                    plane = 48 * (2 * half + deep)
                    own = fmap[
                        plane : plane + 48,
                        pl.ds(pl.multiple_of(i * 4 * LANES + row * LANES, LANES), LANES),
                    ]
                    mpad[
                        plane : plane + 48,
                        pl.ds(pl.multiple_of(i * 4 * LANES + (row + 1) * LANES, LANES), LANES),
                    ] = (part + own.astype(F32)).astype(BF16)
        return 0

    per_seg = seg_rows // 2
    for seg in range(SEGS):
        pooled(seg)[1]()
        lax.fori_loop(seg * seg_rows, (seg + 1) * seg_rows, shift_halo, 0, unroll=True)
        first = max(seg * per_seg - 1, 0)
        last = (seg + 1) * per_seg - (0 if seg == SEGS - 1 else 1)
        lax.fori_loop(first, last, second_conv, 0, unroll=True)

    def third_conv(i, _):
        base = pl.multiple_of(i * 2 * LANES, 2 * LANES)
        patch = jnp.concatenate(
            [
                mpad[
                    48 * plane : 48 * plane + 48,
                    pl.ds(pl.multiple_of(base + b * LANES, LANES), 2 * LANES),
                ]
                for plane in range(4)
                for b in range(3)
            ],
            axis=0,
        )
        acc = jnp.dot(w3_band[...], patch, preferred_element_type=F32)
        lane = lanes_of(72)
        for row in range(2):
            at = slice(row * LANES, (row + 1) * LANES)
            total = (
                acc[72:144, at]
                + lane_shift(acc[0:72, at], 1, lane)
                + lane_shift(acc[144:216, at], -1, lane)
            )
            to = pl.ds(pl.multiple_of(base + row * LANES, LANES), LANES)
            terms[:, to] = total
            edge[0:16, to] = total[0:16].astype(BF16)
            edge[16:32, to] = total[56:72].astype(BF16)
        return 0

    def edges(seg):
        at = pl.ds(pl.multiple_of(seg * BY * LANES, BY * LANES), BY * LANES)
        return exchange(
            edge.at[0:16, at], ehalo.at[16:32, at],
            edge.at[16:32, at], ehalo.at[0:16, at], esend, erecv, seg,
        )

    def third_segment(seg, _):
        lax.fori_loop(
            0, BY // 2, lambda i, _: third_conv(seg * (BY // 2) + i, 0), 0, unroll=True
        )
        edges(seg)[0]()
        return 0

    lax.fori_loop(0, ny // BY, third_segment, 0)

    spread_row = lax.broadcasted_iota(jnp.int32, (BY * LANES, LANES), 0)
    spread_col = lax.broadcasted_iota(jnp.int32, (BY * LANES, LANES), 1)
    spread = jnp.where(
        spread_col == (spread_row // LANES) * BX + lax.rem(spread_row, BX), 1.0, 0.0
    ).astype(BF16)
    block_mask = (
        lax.broadcasted_iota(jnp.int32, (nbx * PART, LANES), 0) // PART
        == lax.broadcasted_iota(jnp.int32, (nbx * PART, LANES), 1) // BX
    )
    directions, channels = wa_ref.shape

    def head_matrix(rows, first_at, second_at):
        across = 3 * rows
        inside = lax.rem(lax.broadcasted_iota(jnp.int32, (channels, across), 1), rows)
        channel = lax.broadcasted_iota(jnp.int32, (channels, across), 0)
        hit = (inside == channel + first_at) | (inside == channel + second_at)
        columns = jnp.dot(
            wa_ref[...], jnp.where(hit, 1.0, 0.0).astype(BF16), preferred_element_type=F32
        ).astype(BF16)
        turn = lax.broadcasted_iota(jnp.int32, (PART, directions), 0) // 2
        turn = turn == lax.broadcasted_iota(jnp.int32, (PART, directions), 1)
        full = jnp.dot(
            jnp.where(turn, 1.0, 0.0).astype(BF16), columns, preferred_element_type=F32
        )
        at = lax.rem(lax.broadcasted_iota(jnp.int32, (PART, across), 1), rows)
        odd = lax.rem(lax.broadcasted_iota(jnp.int32, (PART, across), 0), 2) == 1
        start = jnp.where(odd, second_at, first_at)
        keep = (at >= start) & (at < start + channels)
        return jnp.where(keep, full, 0.0).astype(BF16)

    def head_rows(matrix, total_of):
        def head(by, _):
            parts = []
            for pair in range(BY // 2):
                at = pl.ds(pl.multiple_of((by * BY + 2 * pair) * LANES, LANES), 2 * LANES)
                third = jnp.maximum(total_of(at), 0.0)
                one = third.astype(BF16).astype(F32)
                rest = third - one
                two = rest.astype(BF16).astype(F32)
                three = rest - two
                split = jnp.concatenate([one, two, three], axis=0).astype(BF16)
                logits = jnp.dot(matrix, split, preferred_element_type=F32)
                affinity = 1.0 / (1.0 + jnp.exp(-logits))
                for row in range(2):
                    tile = affinity[:, row * LANES : (row + 1) * LANES]
                    stacked = jnp.concatenate([tile] * nbx, axis=0)
                    parts.append(jnp.where(block_mask, stacked, 0.0).astype(BF16))
            rows = nbx * PART
            masked[pl.ds(pl.multiple_of(by * rows, rows), rows), :] = jnp.concatenate(
                parts, axis=1
            )
            return 0

        return head

    per = SEND_CAP * PART

    def message(part, step):
        target = lax.rem(me + step, n)
        return remote(
            outgoing.at[part, pl.ds(pl.multiple_of(target * per, per), per)],
            out_ref.at[part, me], asend.at[part, step], arecv.at[part, step], target,
        )

    def send_part(part):
        tiles[part] = jnp.dot(masked[...], spread, preferred_element_type=F32).astype(BF16)

        def route(g, _):
            at = pl.ds(pl.multiple_of(g * group, group), group)
            outgoing[part, at, :] = jnp.dot(
                picks[at, :], tiles[part], preferred_element_type=F32
            ).astype(BF16)
            return 0

        def send(step, _):
            message(part, step).start()
            return 0

        lax.fori_loop(0, groups, route, 0)
        lax.fori_loop(1, n, send, 0)
        out_ref[part, me] = outgoing[part, pl.ds(pl.multiple_of(me * per, per), per), :]

    inner_head = head_rows(head_matrix(24, 0, 12), lambda at: terms[24:48, at])
    lax.fori_loop(0, ny // BY, inner_head, 0, unroll=2)
    send_part(0)

    def outer_total(at):
        low = terms[8:24, at] + ehalo[0:16, at].astype(F32)
        high = terms[48:64, at] + ehalo[16:32, at].astype(F32)
        return jnp.concatenate([low, high], axis=0)

    outer_head = head_rows(head_matrix(32, 4, 16), outer_total)

    def outer_segment(by, _):
        edges(by)[1]()
        return outer_head(by, 0)

    lax.fori_loop(0, ny // BY, outer_segment, 0)
    send_part(1)

    features_sent()

    def pooled_sent(seg, _):
        pooled(seg)[2]()
        return 0

    def edges_sent(seg, _):
        edges(seg)[2]()
        return 0

    lax.fori_loop(0, SEGS, pooled_sent, 0)
    lax.fori_loop(0, ny // BY, edges_sent, 0)

    def receive(step, _):
        message(0, step).wait()
        message(1, step).wait()
        return 0

    lax.fori_loop(1, n, receive, 0)


def first_matrix(w_first, depth):
    c1, c0 = w_first.shape[0], w_first.shape[1] // 27
    place = np.zeros((depth, 3, 9, c0, 9, 80), np.float32)
    for z in range(depth):
        for a in range(3):
            for i in range(c0):
                plane = z + a - 1
                if plane < 0:
                    row = i
                elif plane == depth:
                    row = 64 + i
                else:
                    row = 16 + depth * i + plane
                for bc in range(9):
                    place[z, a, bc, i, bc, row] = 1
    place = place.reshape(depth, 27 * c0, 720).astype(ml_dtypes.bfloat16)
    first = jnp.einsum("oi,zik->zok", w_first, place, preferred_element_type=F32)
    return first.astype(BF16).reshape(depth * c1, 720)


def on_device(features, w_first, w_second, w_lift, w_merge, w_affine, tissue, owners):
    n = lax.axis_size("gz")
    channels, depth, ny, nx = features.shape
    cells = ny * nx
    hcells = (ny // 2) * nx
    flat = features.reshape(channels * depth, cells)
    rims = jnp.stack([features[:, 0], features[:, depth - 1]])
    rims = jnp.pad(rims, ((0, 0), (0, 16 - channels), (0, 0), (0, 0))).reshape(32, cells)
    first = first_matrix(w_first, depth)
    per = SEND_CAP * PART
    blocks = (ny // BY) * (nx // BX)
    vmem = pl.BlockSpec(memory_space=pltpu.VMEM)
    routed = pl.pallas_call(
        functools.partial(kernel, n, ny),
        out_shape=jax.ShapeDtypeStruct((2, n, per, LANES), BF16),
        in_specs=[vmem] * 9,
        out_specs=vmem,
        scratch_shapes=[
            pltpu.VMEM((32, cells), BF16),
            pltpu.VMEM((240, cells + 2 * LANES), BF16),
            pltpu.VMEM((192, cells), BF16),
            pltpu.VMEM((576, hcells + 2 * LANES), BF16),
            pltpu.VMEM((192, cells + 2 * LANES), BF16),
            pltpu.VMEM((72, cells), F32),
            pltpu.VMEM((32, cells), BF16),
            pltpu.VMEM((32, cells), BF16),
            pltpu.VMEM((192, 1728), BF16),
            pltpu.VMEM((216, 576), BF16),
            pltpu.VMEM((n * per, blocks * PART), BF16),
            pltpu.VMEM((blocks * PART, BY * LANES), BF16),
            pltpu.VMEM((2, blocks * PART, LANES), BF16),
            pltpu.VMEM((2, n * per, LANES), BF16),
            pltpu.SemaphoreType.DMA((2, 1)),
            pltpu.SemaphoreType.DMA((2, 1)),
            pltpu.SemaphoreType.DMA((2, SEGS)),
            pltpu.SemaphoreType.DMA((2, SEGS)),
            pltpu.SemaphoreType.DMA((2, ny // BY)),
            pltpu.SemaphoreType.DMA((2, ny // BY)),
            pltpu.SemaphoreType.DMA((2, n)),
            pltpu.SemaphoreType.DMA((2, n)),
        ],
        compiler_params=pltpu.CompilerParams(
            collective_id=0, has_side_effects=True, vmem_limit_bytes=48 * 1024 * 1024
        ),
        cost_estimate=pl.CostEstimate(
            flops=1600000000, bytes_accessed=2000000, transcendentals=65536
        ),
    )(flat, rims, first, w_second, w_lift, w_merge, w_affine, tissue, owners)
    directions = w_affine.shape[0]
    routed = routed.reshape(2, n, SEND_CAP, PART // 2, 2, LANES)[:, :, :, :directions]
    routed = jnp.concatenate(
        [routed[1, :, :, :, :1], routed[0], routed[1, :, :, :, 1:]], axis=3
    )
    return routed.reshape(1, n, SEND_CAP, directions * depth * LANES)


def solution(mesh):
    placed = (
        P(None, ("grp", "gz"), None, None),
        P(),
        P(),
        P(),
        P(),
        P(),
        P(("grp", "gz"), None),
        P(("grp", "gz"), None),
    )
    return jax.shard_map(
        on_device,
        mesh=mesh,
        in_specs=placed,
        out_specs=P(("grp", "gz"), None, None, None),
        check_vma=False,
    )
```

```python
import functools

import jax
import jax.numpy as jnp
from jax import lax
from jax.experimental import pallas as pl
from jax.experimental.pallas import tpu as pltpu
from jax.sharding import PartitionSpec as P

BY = 8
BX = 16
SEND_CAP = 2
LANES = 128
PART = 8
SEGS = 4
F32 = jnp.float32
BF16 = jnp.bfloat16


def lane_shift(tile, step, lane):
    rolled = pltpu.roll(tile, step % LANES, axis=1)
    keep = lane >= step if step > 0 else lane < LANES + step
    return jnp.where(keep, rolled, 0.0)


def kernel(
    n, ny,
    f_ref, w1_ref, w2_ref, wl_ref, w3_ref, wa_ref, tissue_ref, owners_ref,
    out_ref,
    rim_ref, w1_band, carry, carry3, landing, fhalo, xpad, fmap, pool, mpad, terms, edge, ehalo, w2_band, w3_band, picks, masked, tiles, outgoing,
    fsend, frecv, psend, precv, esend, erecv, asend, arecv,
):
    me = lax.axis_index("gz")
    has_left = me > 0
    has_right = me < n - 1
    left = me - 1
    right = me + 1
    cells = ny * LANES
    hy = ny // 2
    hcells = hy * LANES

    barrier = pltpu.get_barrier_semaphore()

    def greet(step, _):
        pl.semaphore_signal(
            barrier, inc=1, device_id={"gz": lax.rem(me + step, n)},
            device_id_type=pl.DeviceIdType.MESH,
        )
        return 0

    lax.fori_loop(1, n, greet, 0)

    def lanes_of(rows):
        return lax.broadcasted_iota(jnp.int32, (rows, LANES), 1)

    xpad[:, 0:LANES] = jnp.zeros((240, LANES), BF16)
    xpad[:, cells + LANES : cells + 2 * LANES] = jnp.zeros((240, LANES), BF16)
    pool[:, 0:LANES] = jnp.zeros((576, LANES), BF16)
    pool[:, hcells + LANES : hcells + 2 * LANES] = jnp.zeros((576, LANES), BF16)
    mpad[:, 0:LANES] = jnp.zeros((192, LANES), BF16)
    mpad[:, cells + LANES : cells + 2 * LANES] = jnp.zeros((192, LANES), BF16)

    def remote(src, dst, send, recv, target):
        return pltpu.make_async_remote_copy(
            src_ref=src, dst_ref=dst, send_sem=send, recv_sem=recv,
            device_id={"gz": target}, device_id_type=pl.DeviceIdType.MESH,
        )

    def exchange(to_left, at_right, to_right, at_left, send, recv, seg):
        go_left = remote(to_left, at_right, send.at[0, seg], recv.at[0, seg], left)
        go_right = remote(to_right, at_left, send.at[1, seg], recv.at[1, seg], right)

        def start():
            @pl.when(has_left)
            def _():
                go_left.start()

            @pl.when(has_right)
            def _():
                go_right.start()

        def receive():
            @pl.when(has_right)
            def _():
                go_left.wait_recv()

            @pl.when(has_left)
            def _():
                go_right.wait_recv()

            @pl.when(jnp.logical_not(has_right))
            def _():
                at_right[...] = jnp.zeros(at_right.shape, at_right.dtype)

            @pl.when(jnp.logical_not(has_left))
            def _():
                at_left[...] = jnp.zeros(at_left.shape, at_left.dtype)

        def sent():
            @pl.when(has_left)
            def _():
                go_left.wait_send()

            @pl.when(has_right)
            def _():
                go_right.wait_send()

        return start, receive, sent

    f_rows = f_ref.shape[0]
    depth = 4
    rim_row = lax.broadcasted_iota(jnp.int32, (32, f_rows), 0)
    rim_col = lax.broadcasted_iota(jnp.int32, (32, f_rows), 1)
    rim_at = lax.rem(rim_row, 16) * depth + jnp.where(rim_row < 16, 0, depth - 1)
    rim_pick = jnp.where(rim_at == rim_col, 1.0, 0.0).astype(BF16)
    for at in range(0, cells, 1024):
        rim_ref[:, at : at + 1024] = jnp.dot(
            rim_pick, f_ref[:, at : at + 1024], preferred_element_type=F32
        ).astype(BF16)

    pl.semaphore_wait(barrier, n - 1)

    features_start, features_receive, features_sent = exchange(
        rim_ref.at[0:16], fhalo.at[16:32], rim_ref.at[16:32], fhalo.at[0:16], fsend, frecv, 0
    )
    features_start()

    nbx = LANES // BX
    count = tissue_ref.shape[1]
    blocks = (ny // BY) * nbx
    shape = (count, count)
    r = lax.broadcasted_iota(jnp.int32, shape, 0)
    c = lax.broadcasted_iota(jnp.int32, shape, 1)
    own_row = jnp.broadcast_to(owners_ref[...], shape)
    tis_row = jnp.broadcast_to(tissue_ref[...], shape)
    own_col = jnp.sum(jnp.where(r == c, own_row, 0), axis=1, keepdims=True)
    tis_col = jnp.sum(jnp.where(r == c, tis_row, 0), axis=1, keepdims=True)
    rank = jnp.sum(jnp.where((own_row == own_col) & (c < r), 1, 0), axis=1, keepdims=True)
    slot_col = own_col * SEND_CAP + rank
    wide_shape = (count, blocks * PART)
    block_of = lax.broadcasted_iota(jnp.int32, wide_shape, 1) // PART
    slot_row = (
        jnp.sum(jnp.where(tis_col == block_of, slot_col + 1, 0), axis=0, keepdims=True) - 1
    )
    group = 256

    def pick_rows(g, _):
        row = lax.broadcasted_iota(jnp.int32, (group, blocks * PART), 0) + g * group
        col = lax.broadcasted_iota(jnp.int32, (group, blocks * PART), 1)
        pick = (row // PART == slot_row) & (lax.rem(row, PART) == lax.rem(col, PART))
        picks[pl.ds(pl.multiple_of(g * group, group), group), :] = jnp.where(
            pick, 1.0, 0.0
        ).astype(BF16)
        return 0

    groups = n * SEND_CAP * PART // group
    lax.fori_loop(0, groups, pick_rows, 0)

    w2 = w2_ref[...].astype(F32)
    blank = jnp.zeros((96, 432), F32)
    w2_band[0:96, :] = jnp.concatenate([w2, blank], axis=1).astype(BF16)
    w2_band[96:192, :] = jnp.concatenate([blank, w2], axis=1).astype(BF16)

    taps = w1_ref.shape[1]
    tap = lax.broadcasted_iota(jnp.int32, (1, taps), 1)
    w1 = w1_ref[...].astype(F32)
    by_y = jnp.concatenate(
        [jnp.where(lax.rem(tap // 36, 3) == b, w1, 0.0) for b in range(3)], axis=0
    ).astype(BF16)
    tap = lax.broadcasted_iota(jnp.int32, (taps, 1), 0)
    channel = lax.rem(tap, 12)
    x_off = lax.rem(tap // 12, 3)
    z_off = tap // 108
    target = lax.broadcasted_iota(jnp.int32, (taps, 240), 1)
    for z in range(depth):
        plane = z_off + (z - 1)
        row = jnp.where(
            plane < 0,
            channel,
            jnp.where(plane == depth, 64 + channel, 16 + depth * channel + plane),
        )
        place = jnp.where(target == x_off * 80 + row, 1.0, 0.0).astype(BF16)
        w1_band[144 * z : 144 * z + 144, :] = jnp.dot(
            by_y, place, preferred_element_type=F32
        ).astype(BF16)

    w3 = w3_ref[...].astype(F32)
    bands = []
    for bc in range(9):
        columns = jnp.concatenate(
            [w3[:, (9 * a + bc) * 48 : (9 * a + bc) * 48 + 48] for a in range(3)], axis=1
        )
        for zo in range(6):
            first = 48 * (zo - 2)
            low, high = max(first, 0), min(first + 144, 192)
            pieces = [columns[:, low - first : high - first]]
            if low > 0:
                pieces.insert(0, jnp.zeros((12, low), F32))
            if high < 192:
                pieces.append(jnp.zeros((12, 192 - high), F32))
            bands.append(jnp.concatenate(pieces, axis=1))
    w3_band[...] = jnp.concatenate(bands, axis=0).astype(BF16)

    def shift_rows(v, row0, to):
        rows = v.shape[0]
        lane = lanes_of(rows)
        vf = v.astype(F32)
        xpad[row0 : row0 + rows, to] = lane_shift(vf, 1, lane).astype(BF16)
        xpad[80 + row0 : 80 + row0 + rows, to] = v
        xpad[160 + row0 : 160 + row0 + rows, to] = lane_shift(vf, -1, lane).astype(BF16)

    def shift_own(y, _):
        at = pl.ds(pl.multiple_of(y * LANES, LANES), LANES)
        to = pl.ds(pl.multiple_of((y + 1) * LANES, LANES), LANES)
        shift_rows(f_ref[:, at], 16, to)
        return 0

    lax.fori_loop(0, ny, shift_own, 0, unroll=4)
    features_receive()

    def shift_rims(y, _):
        at = pl.ds(pl.multiple_of(y * LANES, LANES), LANES)
        to = pl.ds(pl.multiple_of((y + 1) * LANES, LANES), LANES)
        shift_rows(fhalo[0:16, at], 0, to)
        shift_rows(fhalo[16:32, at], 64, to)
        return 0

    lax.fori_loop(0, ny, shift_rims, 0, unroll=4)

    def shift_pool(row0, rows, v, to):
        lane = lanes_of(rows)
        pool[row0 : row0 + rows, to] = lane_shift(v, 2, lane).astype(BF16)
        pool[384 + row0 : 384 + row0 + rows, to] = lane_shift(v, -2, lane).astype(BF16)

    def sum_rows(product, offset, held):
        one = slice(0, LANES)
        two = slice(LANES, 2 * LANES)
        done = [
            held[0] + offset(product, 2, one),
            held[1] + offset(product, 1, one) + offset(product, 2, two),
        ]
        held[0] = offset(product, 0, one) + offset(product, 1, two)
        held[1] = offset(product, 0, two)
        return done

    def first_offset(product, b, at):
        return jnp.concatenate(
            [product[144 * z + 48 * b : 144 * z + 48 * b + 48, at] for z in range(depth)], axis=0
        )

    def first_product(pair):
        at = pl.ds(pl.multiple_of(pair * 2 * LANES, 2 * LANES), 2 * LANES)
        return jnp.dot(w1_band[...], xpad[:, at], preferred_element_type=F32)

    carry[...] = jnp.zeros(carry.shape, F32)
    sum_rows(first_product(0), first_offset, carry)

    def first_conv(i, _):
        base = pl.multiple_of(i * 2 * LANES, 2 * LANES)
        acc = jnp.concatenate(sum_rows(first_product(i + 1), first_offset, carry), axis=1)
        acc = jnp.maximum(acc, 0.0)
        fmap[:, pl.ds(base, 2 * LANES)] = acc.astype(BF16)
        deep = jnp.concatenate(
            [jnp.maximum(acc[0:48], acc[48:96]), jnp.maximum(acc[96:144], acc[144:192])], axis=0
        )
        wide = jnp.maximum(deep[:, 0:LANES], deep[:, LANES : 2 * LANES])
        even = lax.rem(lanes_of(96), 2) == 0
        other = jnp.where(
            even, pltpu.roll(wide, LANES - 1, axis=1), pltpu.roll(wide, 1, axis=1)
        )
        both = jnp.maximum(wide, other)
        to = pl.ds(pl.multiple_of((i + 1) * LANES, LANES), LANES)
        pool[240:336, to] = both.astype(BF16)
        shift_pool(48, 96, both, to)
        return 0

    seg_rows = hy // SEGS

    def pooled(seg):
        at = pl.ds(pl.multiple_of((seg * seg_rows + 1) * LANES, LANES), seg_rows * LANES)
        return exchange(
            pool.at[240:288, at], pool.at[336:384, at],
            pool.at[288:336, at], pool.at[192:240, at], psend, precv, seg,
        )

    def first_segment(seg, _):
        lax.fori_loop(
            0, seg_rows, lambda i, _: first_conv(seg * seg_rows + i, 0), 0, unroll=True
        )
        pooled(seg)[0]()
        return 0

    lax.fori_loop(0, SEGS, first_segment, 0)

    def shift_halo(y, _):
        to = pl.ds(pl.multiple_of((y + 1) * LANES, LANES), LANES)
        shift_pool(0, 48, pool[192:240, to].astype(F32), to)
        shift_pool(144, 48, pool[336:384, to].astype(F32), to)
        return 0

    def second_conv(i, _):
        base = pl.multiple_of(i * 2 * LANES, 2 * LANES)
        patch = jnp.concatenate(
            [
                pool[
                    192 * c + 48 * plane : 192 * c + 48 * plane + 48,
                    pl.ds(pl.multiple_of(base + b * LANES, LANES), 2 * LANES),
                ]
                for plane in range(4)
                for b in range(3)
                for c in range(3)
            ],
            axis=0,
        )
        acc = jnp.dot(w2_band[...], patch, preferred_element_type=F32)
        second = jnp.maximum(acc, 0.0).astype(BF16)
        for half in range(2):
            lifted = jnp.dot(
                wl_ref[...], second[96 * half : 96 * half + 96], preferred_element_type=F32
            )
            for row in range(4):
                part = lifted[:, (row // 2) * LANES : (row // 2 + 1) * LANES]
                for deep in range(2):
                    plane = 48 * (2 * half + deep)
                    own = fmap[
                        plane : plane + 48,
                        pl.ds(pl.multiple_of(i * 4 * LANES + row * LANES, LANES), LANES),
                    ]
                    mpad[
                        plane : plane + 48,
                        pl.ds(pl.multiple_of(i * 4 * LANES + (row + 1) * LANES, LANES), LANES),
                    ] = (part + own.astype(F32)).astype(BF16)
        return 0

    per_seg = seg_rows // 2
    for seg in range(SEGS):
        pooled(seg)[1]()
        lax.fori_loop(seg * seg_rows, (seg + 1) * seg_rows, shift_halo, 0, unroll=True)
        first = max(seg * per_seg - 1, 0)
        last = (seg + 1) * per_seg - (0 if seg == SEGS - 1 else 1)
        lax.fori_loop(first, last, second_conv, 0, unroll=True)

    def third_offset(product, b, at):
        return product[216 * b : 216 * b + 216, at]

    def third_product(pair):
        at = pl.ds(pl.multiple_of(pair * 2 * LANES, 2 * LANES), 2 * LANES)
        return jnp.dot(w3_band[...], mpad[:, at], preferred_element_type=F32)

    carry3[...] = jnp.zeros(carry3.shape, F32)
    sum_rows(third_product(0), third_offset, carry3)

    def third_conv(i, _):
        base = pl.multiple_of(i * 2 * LANES, 2 * LANES)
        done = sum_rows(third_product(i + 1), third_offset, carry3)
        lane = lanes_of(72)
        for row in range(2):
            acc = done[row]
            total = (
                acc[72:144] + lane_shift(acc[0:72], 1, lane) + lane_shift(acc[144:216], -1, lane)
            )
            to = pl.ds(pl.multiple_of(base + row * LANES, LANES), LANES)
            terms[:, to] = total
            edge[0:16, to] = total[0:16].astype(BF16)
            edge[16:32, to] = total[56:72].astype(BF16)
        return 0

    def edges(seg):
        at = pl.ds(pl.multiple_of(seg * BY * LANES, BY * LANES), BY * LANES)
        return exchange(
            edge.at[0:16, at], ehalo.at[16:32, at],
            edge.at[16:32, at], ehalo.at[0:16, at], esend, erecv, seg,
        )

    def third_segment(seg, _):
        lax.fori_loop(
            0, BY // 2, lambda i, _: third_conv(seg * (BY // 2) + i, 0), 0, unroll=True
        )
        edges(seg)[0]()
        return 0

    lax.fori_loop(0, ny // BY, third_segment, 0)

    spread_row = lax.broadcasted_iota(jnp.int32, (BY * LANES, LANES), 0)
    spread_col = lax.broadcasted_iota(jnp.int32, (BY * LANES, LANES), 1)
    spread = jnp.where(
        spread_col == (spread_row // LANES) * BX + lax.rem(spread_row, BX), 1.0, 0.0
    ).astype(BF16)
    block_mask = (
        lax.broadcasted_iota(jnp.int32, (nbx * PART, LANES), 0) // PART
        == lax.broadcasted_iota(jnp.int32, (nbx * PART, LANES), 1) // BX
    )
    directions, channels = wa_ref.shape

    def head_matrix(rows, first_at, second_at):
        across = 3 * rows
        inside = lax.rem(lax.broadcasted_iota(jnp.int32, (channels, across), 1), rows)
        channel = lax.broadcasted_iota(jnp.int32, (channels, across), 0)
        hit = (inside == channel + first_at) | (inside == channel + second_at)
        columns = jnp.dot(
            wa_ref[...], jnp.where(hit, 1.0, 0.0).astype(BF16), preferred_element_type=F32
        ).astype(BF16)
        turn = lax.broadcasted_iota(jnp.int32, (PART, directions), 0) // 2
        turn = turn == lax.broadcasted_iota(jnp.int32, (PART, directions), 1)
        full = jnp.dot(
            jnp.where(turn, 1.0, 0.0).astype(BF16), columns, preferred_element_type=F32
        )
        at = lax.rem(lax.broadcasted_iota(jnp.int32, (PART, across), 1), rows)
        odd = lax.rem(lax.broadcasted_iota(jnp.int32, (PART, across), 0), 2) == 1
        start = jnp.where(odd, second_at, first_at)
        keep = (at >= start) & (at < start + channels)
        return jnp.where(keep, full, 0.0).astype(BF16)

    def head_rows(matrix, total_of):
        def head(by, _):
            parts = []
            for pair in range(BY // 2):
                at = pl.ds(pl.multiple_of((by * BY + 2 * pair) * LANES, LANES), 2 * LANES)
                third = jnp.maximum(total_of(at), 0.0)
                one = third.astype(BF16).astype(F32)
                rest = third - one
                two = rest.astype(BF16).astype(F32)
                three = rest - two
                split = jnp.concatenate([one, two, three], axis=0).astype(BF16)
                logits = jnp.dot(matrix, split, preferred_element_type=F32)
                affinity = 1.0 / (1.0 + jnp.exp(-logits))
                for row in range(2):
                    tile = affinity[:, row * LANES : (row + 1) * LANES]
                    stacked = jnp.concatenate([tile] * nbx, axis=0)
                    parts.append(jnp.where(block_mask, stacked, 0.0).astype(BF16))
            rows = nbx * PART
            masked[pl.ds(pl.multiple_of(by * rows, rows), rows), :] = jnp.concatenate(
                parts, axis=1
            )
            return 0

        return head

    per = SEND_CAP * PART

    def message(part, step):
        target = lax.rem(me + step, n)
        return remote(
            outgoing.at[part, pl.ds(pl.multiple_of(target * per, per), per)],
            landing.at[part, me], asend.at[part, step], arecv.at[part, step], target,
        )

    def send_part(part):
        tiles[part] = jnp.dot(masked[...], spread, preferred_element_type=F32).astype(BF16)

        def route(g, _):
            at = pl.ds(pl.multiple_of(g * group, group), group)
            outgoing[part, at, :] = jnp.dot(
                picks[at, :], tiles[part], preferred_element_type=F32
            ).astype(BF16)
            return 0

        def send(step, _):
            message(part, step).start()
            return 0

        lax.fori_loop(0, groups, route, 0)
        lax.fori_loop(1, n, send, 0)
        landing[part, me] = outgoing[part, pl.ds(pl.multiple_of(me * per, per), per), :]

    inner_head = head_rows(head_matrix(24, 0, 12), lambda at: terms[24:48, at])
    lax.fori_loop(0, ny // BY, inner_head, 0, unroll=2)
    send_part(0)

    def outer_total(at):
        low = terms[8:24, at] + ehalo[0:16, at].astype(F32)
        high = terms[48:64, at] + ehalo[16:32, at].astype(F32)
        return jnp.concatenate([low, high], axis=0)

    outer_head = head_rows(head_matrix(32, 4, 16), outer_total)

    def outer_segment(by, _):
        edges(by)[1]()
        return outer_head(by, 0)

    lax.fori_loop(0, ny // BY, outer_segment, 0)
    send_part(1)

    features_sent()

    def pooled_sent(seg, _):
        pooled(seg)[2]()
        return 0

    def edges_sent(seg, _):
        edges(seg)[2]()
        return 0

    lax.fori_loop(0, SEGS, pooled_sent, 0)
    lax.fori_loop(0, ny // BY, edges_sent, 0)

    def receive(step, _):
        message(0, step).wait()
        message(1, step).wait()
        return 0

    lax.fori_loop(1, n, receive, 0)

    slots = n * SEND_CAP
    used = 2 * directions
    line = lax.broadcasted_iota(jnp.int32, (used * slots, slots * PART), 0)
    source = lax.rem(line, slots) * PART + line // slots
    gather = jnp.where(
        source == lax.broadcasted_iota(jnp.int32, (used * slots, slots * PART), 1), 1.0, 0.0
    ).astype(BF16)
    inner_rows, outer_rows = [
        jnp.dot(
            gather, landing[part].reshape(slots * PART, LANES), preferred_element_type=F32
        )
        for part in range(2)
    ]
    lines = []
    for d in range(directions):
        for rows_of, turn in ((outer_rows, 0), (inner_rows, 0), (inner_rows, 1), (outer_rows, 1)):
            k = (2 * d + turn) * slots
            lines.append(rows_of[k : k + slots])
    whole = jnp.concatenate(lines, axis=1)
    for s in range(n):
        out_ref[s] = whole[SEND_CAP * s : SEND_CAP * s + SEND_CAP].astype(BF16)


def on_device(features, w_first, w_second, w_lift, w_merge, w_affine, tissue, owners):
    n = lax.axis_size("gz")
    channels, depth, ny, nx = features.shape
    cells = ny * nx
    hcells = (ny // 2) * nx
    flat = features.reshape(channels * depth, cells)
    per = SEND_CAP * PART
    blocks = (ny // BY) * (nx // BX)
    vmem = pl.BlockSpec(memory_space=pltpu.VMEM)
    routed = pl.pallas_call(
        functools.partial(kernel, n, ny),
        out_shape=jax.ShapeDtypeStruct((n, SEND_CAP, w_affine.shape[0] * depth * LANES), BF16),
        in_specs=[vmem] * 8,
        out_specs=vmem,
        scratch_shapes=[
            pltpu.VMEM((32, cells), BF16),
            pltpu.VMEM((576, 240), BF16),
            pltpu.VMEM((2, 192, LANES), F32),
            pltpu.VMEM((2, 216, LANES), F32),
            pltpu.VMEM((2, n, per, LANES), BF16),
            pltpu.VMEM((32, cells), BF16),
            pltpu.VMEM((240, cells + 2 * LANES), BF16),
            pltpu.VMEM((192, cells), BF16),
            pltpu.VMEM((576, hcells + 2 * LANES), BF16),
            pltpu.VMEM((192, cells + 2 * LANES), BF16),
            pltpu.VMEM((72, cells), F32),
            pltpu.VMEM((32, cells), BF16),
            pltpu.VMEM((32, cells), BF16),
            pltpu.VMEM((192, 1728), BF16),
            pltpu.VMEM((648, 192), BF16),
            pltpu.VMEM((n * per, blocks * PART), BF16),
            pltpu.VMEM((blocks * PART, BY * LANES), BF16),
            pltpu.VMEM((2, blocks * PART, LANES), BF16),
            pltpu.VMEM((2, n * per, LANES), BF16),
            pltpu.SemaphoreType.DMA((2, 1)),
            pltpu.SemaphoreType.DMA((2, 1)),
            pltpu.SemaphoreType.DMA((2, SEGS)),
            pltpu.SemaphoreType.DMA((2, SEGS)),
            pltpu.SemaphoreType.DMA((2, ny // BY)),
            pltpu.SemaphoreType.DMA((2, ny // BY)),
            pltpu.SemaphoreType.DMA((2, n)),
            pltpu.SemaphoreType.DMA((2, n)),
        ],
        compiler_params=pltpu.CompilerParams(
            collective_id=0, has_side_effects=True, vmem_limit_bytes=48 * 1024 * 1024
        ),
        cost_estimate=pl.CostEstimate(
            flops=1600000000, bytes_accessed=2000000, transcendentals=65536
        ),
    )(flat, w_first, w_second, w_lift, w_merge, w_affine, tissue, owners)
    return routed[None]


def solution(mesh):
    placed = (
        P(None, ("grp", "gz"), None, None),
        P(),
        P(),
        P(),
        P(),
        P(),
        P(("grp", "gz"), None),
        P(("grp", "gz"), None),
    )
    return jax.shard_map(
        on_device,
        mesh=mesh,
        in_specs=placed,
        out_specs=P(("grp", "gz"), None, None, None),
        check_vma=False,
    )
```

```python
import functools

import jax
import jax.numpy as jnp
from jax import lax
from jax.experimental import pallas as pl
from jax.experimental.pallas import tpu as pltpu
from jax.sharding import PartitionSpec as P

BY = 8
BX = 16
SEND_CAP = 2
LANES = 128
PART = 8
SEGS = 4
F32 = jnp.float32
BF16 = jnp.bfloat16


def lane_shift(tile, step, lane):
    rolled = pltpu.roll(tile, step % LANES, axis=1)
    keep = lane >= step if step > 0 else lane < LANES + step
    return jnp.where(keep, rolled, 0.0)


def kernel(
    n, ny,
    f_in, w1_in, w2_in, wl_in, w3_in, wa_in, tissue_in, owners_in,
    out_ref,
    f_ref, w1_ref, w2_ref, wl_ref, w3_ref, wa_ref, tissue_ref, owners_ref, own_sem, planes,
    rim_ref, w1_band, carry, carry3, landing, fhalo, xpad, fmap, pool, mpad, terms, edge, ehalo, w2_band, w3_band, picks, masked, tiles, outgoing,
    fsend, frecv, psend, precv, esend, erecv, asend, arecv,
):
    me = lax.axis_index("gz")
    has_left = me > 0
    has_right = me < n - 1
    left = me - 1
    right = me + 1
    cells = ny * LANES
    hy = ny // 2
    hcells = hy * LANES

    sources = (f_in, w1_in, w2_in, wl_in, w3_in, wa_in, tissue_in, owners_in)
    held_here = (f_ref, w1_ref, w2_ref, wl_ref, w3_ref, wa_ref, tissue_ref, owners_ref)
    loads = [
        pltpu.make_async_copy(source, place, own_sem.at[k])
        for k, (source, place) in enumerate(zip(sources, held_here))
    ]
    for load in loads:
        load.start()

    barrier = pltpu.get_barrier_semaphore()

    def greet(step, _):
        pl.semaphore_signal(
            barrier, inc=1, device_id={"gz": lax.rem(me + step, n)},
            device_id_type=pl.DeviceIdType.MESH,
        )
        return 0

    lax.fori_loop(1, n, greet, 0)

    def lanes_of(rows):
        return lax.broadcasted_iota(jnp.int32, (rows, LANES), 1)

    xpad[:, 0:LANES] = jnp.zeros((240, LANES), BF16)
    xpad[:, cells + LANES : cells + 2 * LANES] = jnp.zeros((240, LANES), BF16)
    pool[:, 0:LANES] = jnp.zeros((576, LANES), BF16)
    pool[:, hcells + LANES : hcells + 2 * LANES] = jnp.zeros((576, LANES), BF16)
    mpad[:, 0:LANES] = jnp.zeros((192, LANES), BF16)
    mpad[:, cells + LANES : cells + 2 * LANES] = jnp.zeros((192, LANES), BF16)

    def remote(src, dst, send, recv, target):
        return pltpu.make_async_remote_copy(
            src_ref=src, dst_ref=dst, send_sem=send, recv_sem=recv,
            device_id={"gz": target}, device_id_type=pl.DeviceIdType.MESH,
        )

    def exchange(to_left, at_right, to_right, at_left, send, recv, seg):
        go_left = remote(to_left, at_right, send.at[0, seg], recv.at[0, seg], left)
        go_right = remote(to_right, at_left, send.at[1, seg], recv.at[1, seg], right)

        def start():
            @pl.when(has_left)
            def _():
                go_left.start()

            @pl.when(has_right)
            def _():
                go_right.start()

        def receive():
            @pl.when(has_right)
            def _():
                go_left.wait_recv()

            @pl.when(has_left)
            def _():
                go_right.wait_recv()

            @pl.when(jnp.logical_not(has_right))
            def _():
                at_right[...] = jnp.zeros(at_right.shape, at_right.dtype)

            @pl.when(jnp.logical_not(has_left))
            def _():
                at_left[...] = jnp.zeros(at_left.shape, at_left.dtype)

        def sent():
            @pl.when(has_left)
            def _():
                go_left.wait_send()

            @pl.when(has_right)
            def _():
                go_right.wait_send()

        return start, receive, sent

    depth = 4
    f_rows = f_ref.shape[0]
    channels_in = f_rows // depth
    loads[0].wait()
    planes[...] = f_ref[...].reshape(f_rows * ny, LANES).astype(F32)
    rim_pad = jnp.zeros((16 - channels_in, LANES), F32)
    for y in range(ny):
        at = slice(y * LANES, (y + 1) * LANES)
        for side in range(2):
            rim = planes[pl.ds(side * (depth - 1) * ny + y, channels_in, stride=depth * ny), :]
            rim_ref[16 * side : 16 * side + 16, at] = jnp.concatenate(
                [rim, rim_pad], axis=0
            ).astype(BF16)

    pl.semaphore_wait(barrier, n - 1)

    features_start, features_receive, features_sent = exchange(
        rim_ref.at[0:16], fhalo.at[16:32], rim_ref.at[16:32], fhalo.at[0:16], fsend, frecv, 0
    )
    features_start()
    for load in loads[1:]:
        load.wait()

    nbx = LANES // BX
    count = tissue_ref.shape[1]
    blocks = (ny // BY) * nbx
    shape = (count, count)
    r = lax.broadcasted_iota(jnp.int32, shape, 0)
    c = lax.broadcasted_iota(jnp.int32, shape, 1)
    own_row = jnp.broadcast_to(owners_ref[...], shape)
    tis_row = jnp.broadcast_to(tissue_ref[...], shape)
    own_col = jnp.sum(jnp.where(r == c, own_row, 0), axis=1, keepdims=True)
    tis_col = jnp.sum(jnp.where(r == c, tis_row, 0), axis=1, keepdims=True)
    rank = jnp.sum(jnp.where((own_row == own_col) & (c < r), 1, 0), axis=1, keepdims=True)
    slot_col = own_col * SEND_CAP + rank
    wide_shape = (count, blocks * PART)
    block_of = lax.broadcasted_iota(jnp.int32, wide_shape, 1) // PART
    slot_row = (
        jnp.sum(jnp.where(tis_col == block_of, slot_col + 1, 0), axis=0, keepdims=True) - 1
    )
    group = 256

    def pick_rows(g, _):
        row = lax.broadcasted_iota(jnp.int32, (group, blocks * PART), 0) + g * group
        col = lax.broadcasted_iota(jnp.int32, (group, blocks * PART), 1)
        pick = (row // PART == slot_row) & (lax.rem(row, PART) == lax.rem(col, PART))
        picks[pl.ds(pl.multiple_of(g * group, group), group), :] = jnp.where(
            pick, 1.0, 0.0
        ).astype(BF16)
        return 0

    groups = n * SEND_CAP * PART // group
    lax.fori_loop(0, groups, pick_rows, 0)

    w2 = w2_ref[...].astype(F32)
    blank = jnp.zeros((96, 432), F32)
    w2_band[0:96, :] = jnp.concatenate([w2, blank], axis=1).astype(BF16)
    w2_band[96:192, :] = jnp.concatenate([blank, w2], axis=1).astype(BF16)

    taps = w1_ref.shape[1]
    tap = lax.broadcasted_iota(jnp.int32, (1, taps), 1)
    w1 = w1_ref[...].astype(F32)
    by_y = jnp.concatenate(
        [jnp.where(lax.rem(tap // 36, 3) == b, w1, 0.0) for b in range(3)], axis=0
    ).astype(BF16)
    tap = lax.broadcasted_iota(jnp.int32, (taps, 1), 0)
    channel = lax.rem(tap, 12)
    x_off = lax.rem(tap // 12, 3)
    z_off = tap // 108
    target = lax.broadcasted_iota(jnp.int32, (taps, 240), 1)
    for z in range(depth):
        plane = z_off + (z - 1)
        row = jnp.where(
            plane < 0,
            channel,
            jnp.where(plane == depth, 64 + channel, 16 + depth * channel + plane),
        )
        place = jnp.where(target == x_off * 80 + row, 1.0, 0.0).astype(BF16)
        w1_band[144 * z : 144 * z + 144, :] = jnp.dot(
            by_y, place, preferred_element_type=F32
        ).astype(BF16)

    w3 = w3_ref[...].astype(F32)
    bands = []
    for bc in range(9):
        columns = jnp.concatenate(
            [w3[:, (9 * a + bc) * 48 : (9 * a + bc) * 48 + 48] for a in range(3)], axis=1
        )
        for zo in range(6):
            first = 48 * (zo - 2)
            low, high = max(first, 0), min(first + 144, 192)
            pieces = [columns[:, low - first : high - first]]
            if low > 0:
                pieces.insert(0, jnp.zeros((12, low), F32))
            if high < 192:
                pieces.append(jnp.zeros((12, 192 - high), F32))
            bands.append(jnp.concatenate(pieces, axis=1))
    w3_band[...] = jnp.concatenate(bands, axis=0).astype(BF16)

    def shift_rows(vf, row0, to):
        rows = vf.shape[0]
        lane = lanes_of(rows)
        xpad[row0 : row0 + rows, to] = lane_shift(vf, 1, lane).astype(BF16)
        xpad[80 + row0 : 80 + row0 + rows, to] = vf.astype(BF16)
        xpad[160 + row0 : 160 + row0 + rows, to] = lane_shift(vf, -1, lane).astype(BF16)

    for y in range(ny):
        shift_rows(
            planes[pl.ds(y, f_rows, stride=ny), :], 16, slice((y + 1) * LANES, (y + 2) * LANES)
        )
    features_receive()

    def shift_rims(y, _):
        at = pl.ds(pl.multiple_of(y * LANES, LANES), LANES)
        to = pl.ds(pl.multiple_of((y + 1) * LANES, LANES), LANES)
        shift_rows(fhalo[0:16, at].astype(F32), 0, to)
        shift_rows(fhalo[16:32, at].astype(F32), 64, to)
        return 0

    lax.fori_loop(0, ny, shift_rims, 0, unroll=4)

    def shift_pool(row0, rows, v, to):
        lane = lanes_of(rows)
        pool[row0 : row0 + rows, to] = lane_shift(v, 2, lane).astype(BF16)
        pool[384 + row0 : 384 + row0 + rows, to] = lane_shift(v, -2, lane).astype(BF16)

    def sum_rows(product, offset, held):
        one = slice(0, LANES)
        two = slice(LANES, 2 * LANES)
        done = [
            held[0] + offset(product, 2, one),
            held[1] + offset(product, 1, one) + offset(product, 2, two),
        ]
        held[0] = offset(product, 0, one) + offset(product, 1, two)
        held[1] = offset(product, 0, two)
        return done

    def first_offset(product, b, at):
        return jnp.concatenate(
            [product[144 * z + 48 * b : 144 * z + 48 * b + 48, at] for z in range(depth)], axis=0
        )

    def first_product(pair):
        at = pl.ds(pl.multiple_of(pair * 2 * LANES, 2 * LANES), 2 * LANES)
        return jnp.dot(w1_band[...], xpad[:, at], preferred_element_type=F32)

    carry[...] = jnp.zeros(carry.shape, F32)
    sum_rows(first_product(0), first_offset, carry)

    def first_conv(i, _):
        base = pl.multiple_of(i * 2 * LANES, 2 * LANES)
        acc = jnp.concatenate(sum_rows(first_product(i + 1), first_offset, carry), axis=1)
        acc = jnp.maximum(acc, 0.0)
        fmap[:, pl.ds(base, 2 * LANES)] = acc.astype(BF16)
        deep = jnp.concatenate(
            [jnp.maximum(acc[0:48], acc[48:96]), jnp.maximum(acc[96:144], acc[144:192])], axis=0
        )
        wide = jnp.maximum(deep[:, 0:LANES], deep[:, LANES : 2 * LANES])
        even = lax.rem(lanes_of(96), 2) == 0
        other = jnp.where(
            even, pltpu.roll(wide, LANES - 1, axis=1), pltpu.roll(wide, 1, axis=1)
        )
        both = jnp.maximum(wide, other)
        to = pl.ds(pl.multiple_of((i + 1) * LANES, LANES), LANES)
        pool[240:336, to] = both.astype(BF16)
        shift_pool(48, 96, both, to)
        return 0

    seg_rows = hy // SEGS

    def pooled(seg):
        at = pl.ds(pl.multiple_of((seg * seg_rows + 1) * LANES, LANES), seg_rows * LANES)
        return exchange(
            pool.at[240:288, at], pool.at[336:384, at],
            pool.at[288:336, at], pool.at[192:240, at], psend, precv, seg,
        )

    def first_segment(seg, _):
        lax.fori_loop(
            0, seg_rows, lambda i, _: first_conv(seg * seg_rows + i, 0), 0, unroll=True
        )
        pooled(seg)[0]()
        return 0

    lax.fori_loop(0, SEGS, first_segment, 0)

    def shift_halo(y, _):
        to = pl.ds(pl.multiple_of((y + 1) * LANES, LANES), LANES)
        shift_pool(0, 48, pool[192:240, to].astype(F32), to)
        shift_pool(144, 48, pool[336:384, to].astype(F32), to)
        return 0

    def second_conv(i, _):
        base = pl.multiple_of(i * 2 * LANES, 2 * LANES)
        patch = jnp.concatenate(
            [
                pool[
                    192 * c + 48 * plane : 192 * c + 48 * plane + 48,
                    pl.ds(pl.multiple_of(base + b * LANES, LANES), 2 * LANES),
                ]
                for plane in range(4)
                for b in range(3)
                for c in range(3)
            ],
            axis=0,
        )
        acc = jnp.dot(w2_band[...], patch, preferred_element_type=F32)
        second = jnp.maximum(acc, 0.0).astype(BF16)
        for half in range(2):
            lifted = jnp.dot(
                wl_ref[...], second[96 * half : 96 * half + 96], preferred_element_type=F32
            )
            for row in range(4):
                part = lifted[:, (row // 2) * LANES : (row // 2 + 1) * LANES]
                for deep in range(2):
                    plane = 48 * (2 * half + deep)
                    own = fmap[
                        plane : plane + 48,
                        pl.ds(pl.multiple_of(i * 4 * LANES + row * LANES, LANES), LANES),
                    ]
                    mpad[
                        plane : plane + 48,
                        pl.ds(pl.multiple_of(i * 4 * LANES + (row + 1) * LANES, LANES), LANES),
                    ] = (part + own.astype(F32)).astype(BF16)
        return 0

    per_seg = seg_rows // 2
    for seg in range(SEGS):
        pooled(seg)[1]()
        lax.fori_loop(seg * seg_rows, (seg + 1) * seg_rows, shift_halo, 0, unroll=True)
        first = max(seg * per_seg - 1, 0)
        last = (seg + 1) * per_seg - (0 if seg == SEGS - 1 else 1)
        lax.fori_loop(first, last, second_conv, 0, unroll=True)

    def third_offset(product, b, at):
        return product[216 * b : 216 * b + 216, at]

    def third_product(pair):
        at = pl.ds(pl.multiple_of(pair * 2 * LANES, 2 * LANES), 2 * LANES)
        return jnp.dot(w3_band[...], mpad[:, at], preferred_element_type=F32)

    carry3[...] = jnp.zeros(carry3.shape, F32)
    sum_rows(third_product(0), third_offset, carry3)

    def third_conv(i, _):
        base = pl.multiple_of(i * 2 * LANES, 2 * LANES)
        done = sum_rows(third_product(i + 1), third_offset, carry3)
        lane = lanes_of(72)
        for row in range(2):
            acc = done[row]
            total = (
                acc[72:144] + lane_shift(acc[0:72], 1, lane) + lane_shift(acc[144:216], -1, lane)
            )
            to = pl.ds(pl.multiple_of(base + row * LANES, LANES), LANES)
            terms[:, to] = total
            edge[0:16, to] = total[0:16].astype(BF16)
            edge[16:32, to] = total[56:72].astype(BF16)
        return 0

    def edges(seg):
        at = pl.ds(pl.multiple_of(seg * BY * LANES, BY * LANES), BY * LANES)
        return exchange(
            edge.at[0:16, at], ehalo.at[16:32, at],
            edge.at[16:32, at], ehalo.at[0:16, at], esend, erecv, seg,
        )

    def third_segment(seg, _):
        lax.fori_loop(
            0, BY // 2, lambda i, _: third_conv(seg * (BY // 2) + i, 0), 0, unroll=True
        )
        edges(seg)[0]()
        return 0

    lax.fori_loop(0, ny // BY, third_segment, 0)

    spread_row = lax.broadcasted_iota(jnp.int32, (BY * LANES, LANES), 0)
    spread_col = lax.broadcasted_iota(jnp.int32, (BY * LANES, LANES), 1)
    spread = jnp.where(
        spread_col == (spread_row // LANES) * BX + lax.rem(spread_row, BX), 1.0, 0.0
    ).astype(BF16)
    block_mask = (
        lax.broadcasted_iota(jnp.int32, (nbx * PART, LANES), 0) // PART
        == lax.broadcasted_iota(jnp.int32, (nbx * PART, LANES), 1) // BX
    )
    directions, channels = wa_ref.shape

    def head_matrix(rows, first_at, second_at):
        across = 3 * rows
        inside = lax.rem(lax.broadcasted_iota(jnp.int32, (channels, across), 1), rows)
        channel = lax.broadcasted_iota(jnp.int32, (channels, across), 0)
        hit = (inside == channel + first_at) | (inside == channel + second_at)
        columns = jnp.dot(
            wa_ref[...], jnp.where(hit, 1.0, 0.0).astype(BF16), preferred_element_type=F32
        ).astype(BF16)
        turn = lax.broadcasted_iota(jnp.int32, (PART, directions), 0) // 2
        turn = turn == lax.broadcasted_iota(jnp.int32, (PART, directions), 1)
        full = jnp.dot(
            jnp.where(turn, 1.0, 0.0).astype(BF16), columns, preferred_element_type=F32
        )
        at = lax.rem(lax.broadcasted_iota(jnp.int32, (PART, across), 1), rows)
        odd = lax.rem(lax.broadcasted_iota(jnp.int32, (PART, across), 0), 2) == 1
        start = jnp.where(odd, second_at, first_at)
        keep = (at >= start) & (at < start + channels)
        return jnp.where(keep, full, 0.0).astype(BF16)

    def head_rows(matrix, total_of):
        def head(by, _):
            parts = []
            for pair in range(BY // 2):
                at = pl.ds(pl.multiple_of((by * BY + 2 * pair) * LANES, LANES), 2 * LANES)
                third = jnp.maximum(total_of(at), 0.0)
                one = third.astype(BF16).astype(F32)
                rest = third - one
                two = rest.astype(BF16).astype(F32)
                three = rest - two
                split = jnp.concatenate([one, two, three], axis=0).astype(BF16)
                logits = jnp.dot(matrix, split, preferred_element_type=F32)
                affinity = 1.0 / (1.0 + jnp.exp(-logits))
                for row in range(2):
                    tile = affinity[:, row * LANES : (row + 1) * LANES]
                    stacked = jnp.concatenate([tile] * nbx, axis=0)
                    parts.append(jnp.where(block_mask, stacked, 0.0).astype(BF16))
            rows = nbx * PART
            masked[pl.ds(pl.multiple_of(by * rows, rows), rows), :] = jnp.concatenate(
                parts, axis=1
            )
            return 0

        return head

    per = SEND_CAP * PART

    def message(part, step):
        target = lax.rem(me + step, n)
        return remote(
            outgoing.at[part, pl.ds(pl.multiple_of(target * per, per), per)],
            landing.at[part, me], asend.at[part, step], arecv.at[part, step], target,
        )

    def send_part(part):
        tiles[part] = jnp.dot(masked[...], spread, preferred_element_type=F32).astype(BF16)

        def route(g, _):
            at = pl.ds(pl.multiple_of(g * group, group), group)
            outgoing[part, at, :] = jnp.dot(
                picks[at, :], tiles[part], preferred_element_type=F32
            ).astype(BF16)
            return 0

        def send(step, _):
            message(part, step).start()
            return 0

        lax.fori_loop(0, groups, route, 0)
        lax.fori_loop(1, n, send, 0)
        landing[part, me] = outgoing[part, pl.ds(pl.multiple_of(me * per, per), per), :]

    inner_head = head_rows(head_matrix(24, 0, 12), lambda at: terms[24:48, at])
    lax.fori_loop(0, ny // BY, inner_head, 0, unroll=2)
    send_part(0)

    def outer_total(at):
        low = terms[8:24, at] + ehalo[0:16, at].astype(F32)
        high = terms[48:64, at] + ehalo[16:32, at].astype(F32)
        return jnp.concatenate([low, high], axis=0)

    outer_head = head_rows(head_matrix(32, 4, 16), outer_total)

    def outer_segment(by, _):
        edges(by)[1]()
        return outer_head(by, 0)

    lax.fori_loop(0, ny // BY, outer_segment, 0)
    send_part(1)

    features_sent()

    def pooled_sent(seg, _):
        pooled(seg)[2]()
        return 0

    def edges_sent(seg, _):
        edges(seg)[2]()
        return 0

    lax.fori_loop(0, SEGS, pooled_sent, 0)
    lax.fori_loop(0, ny // BY, edges_sent, 0)

    def receive(step, _):
        message(0, step).wait()
        message(1, step).wait()
        return 0

    lax.fori_loop(1, n, receive, 0)

    slots = n * SEND_CAP
    used = 2 * directions
    line = lax.broadcasted_iota(jnp.int32, (used * slots, slots * PART), 0)
    source = lax.rem(line, slots) * PART + line // slots
    gather = jnp.where(
        source == lax.broadcasted_iota(jnp.int32, (used * slots, slots * PART), 1), 1.0, 0.0
    ).astype(BF16)
    inner_rows, outer_rows = [
        jnp.dot(
            gather, landing[part].reshape(slots * PART, LANES), preferred_element_type=F32
        )
        for part in range(2)
    ]
    lines = []
    for d in range(directions):
        for rows_of, turn in ((outer_rows, 0), (inner_rows, 0), (inner_rows, 1), (outer_rows, 1)):
            k = (2 * d + turn) * slots
            lines.append(rows_of[k : k + slots])
    whole = jnp.concatenate(lines, axis=1)
    for s in range(n):
        out_ref[s] = whole[SEND_CAP * s : SEND_CAP * s + SEND_CAP].astype(BF16)


def on_device(features, w_first, w_second, w_lift, w_merge, w_affine, tissue, owners):
    n = lax.axis_size("gz")
    channels, depth, ny, nx = features.shape
    cells = ny * nx
    hcells = (ny // 2) * nx
    flat = features.reshape(channels * depth, ny, nx)
    operands = (flat, w_first, w_second, w_lift, w_merge, w_affine, tissue, owners)
    per = SEND_CAP * PART
    blocks = (ny // BY) * (nx // BX)
    vmem = pl.BlockSpec(memory_space=pltpu.VMEM)
    routed = pl.pallas_call(
        functools.partial(kernel, n, ny),
        out_shape=jax.ShapeDtypeStruct((n, SEND_CAP, w_affine.shape[0] * depth * LANES), BF16),
        in_specs=[pl.BlockSpec(memory_space=pltpu.HBM)] * len(operands),
        out_specs=vmem,
        scratch_shapes=[
            *[pltpu.VMEM(operand.shape, operand.dtype) for operand in operands],
            pltpu.SemaphoreType.DMA((len(operands),)),
            pltpu.VMEM((channels * depth * ny, LANES), F32),
            pltpu.VMEM((32, cells), BF16),
            pltpu.VMEM((576, 240), BF16),
            pltpu.VMEM((2, 192, LANES), F32),
            pltpu.VMEM((2, 216, LANES), F32),
            pltpu.VMEM((2, n, per, LANES), BF16),
            pltpu.VMEM((32, cells), BF16),
            pltpu.VMEM((240, cells + 2 * LANES), BF16),
            pltpu.VMEM((192, cells), BF16),
            pltpu.VMEM((576, hcells + 2 * LANES), BF16),
            pltpu.VMEM((192, cells + 2 * LANES), BF16),
            pltpu.VMEM((72, cells), F32),
            pltpu.VMEM((32, cells), BF16),
            pltpu.VMEM((32, cells), BF16),
            pltpu.VMEM((192, 1728), BF16),
            pltpu.VMEM((648, 192), BF16),
            pltpu.VMEM((n * per, blocks * PART), BF16),
            pltpu.VMEM((blocks * PART, BY * LANES), BF16),
            pltpu.VMEM((2, blocks * PART, LANES), BF16),
            pltpu.VMEM((2, n * per, LANES), BF16),
            pltpu.SemaphoreType.DMA((2, 1)),
            pltpu.SemaphoreType.DMA((2, 1)),
            pltpu.SemaphoreType.DMA((2, SEGS)),
            pltpu.SemaphoreType.DMA((2, SEGS)),
            pltpu.SemaphoreType.DMA((2, ny // BY)),
            pltpu.SemaphoreType.DMA((2, ny // BY)),
            pltpu.SemaphoreType.DMA((2, n)),
            pltpu.SemaphoreType.DMA((2, n)),
        ],
        compiler_params=pltpu.CompilerParams(
            collective_id=0, has_side_effects=True, vmem_limit_bytes=63 * 1024 * 1024
        ),
        cost_estimate=pl.CostEstimate(
            flops=1600000000, bytes_accessed=2000000, transcendentals=65536
        ),
    )(*operands)
    return routed[None]


def solution(mesh):
    placed = (
        P(None, ("grp", "gz"), None, None),
        P(),
        P(),
        P(),
        P(),
        P(),
        P(("grp", "gz"), None),
        P(("grp", "gz"), None),
    )
    return jax.shard_map(
        on_device,
        mesh=mesh,
        in_specs=placed,
        out_specs=P(("grp", "gz"), None, None, None),
        check_vma=False,
    )
```

```python
import functools

import jax
import jax.numpy as jnp
from jax import lax
from jax.experimental import pallas as pl
from jax.experimental.pallas import tpu as pltpu
from jax.sharding import PartitionSpec as P

BY = 8
BX = 16
SEND_CAP = 2
LANES = 128
PART = 8
SEGS = 4
F32 = jnp.float32
BF16 = jnp.bfloat16


def lane_shift(tile, step, lane):
    rolled = pltpu.roll(tile, step % LANES, axis=1)
    keep = lane >= step if step > 0 else lane < LANES + step
    return jnp.where(keep, rolled, 0.0)


def kernel(
    n, ny,
    f_in, w1_in, w2_in, wl_in, w3_in, wa_in, tissue_in, owners_in,
    out_ref,
    f_ref, w1_ref, w2_ref, wl_ref, w3_ref, wa_ref, tissue_ref, owners_ref, own_sem, planes,
    rim_ref, w1_band, carry, carry3, landing, fhalo, xpad, fmap, rows_max, pool, shares, mpad, terms, edge, ehalo, w2_band, w3_band, picks, masked, tiles, outgoing,
    fsend, frecv, psend, precv, esend, erecv, asend, arecv,
):
    me = lax.axis_index("gz")
    has_left = me > 0
    has_right = me < n - 1
    left = me - 1
    right = me + 1
    cells = ny * LANES
    hy = ny // 2
    hcells = hy * LANES

    sources = (f_in, w1_in, w2_in, wl_in, w3_in, wa_in, tissue_in, owners_in)
    held_here = (f_ref, w1_ref, w2_ref, wl_ref, w3_ref, wa_ref, tissue_ref, owners_ref)
    loads = [
        pltpu.make_async_copy(source, place, own_sem.at[k])
        for k, (source, place) in enumerate(zip(sources, held_here))
    ]
    for load in loads:
        load.start()

    barrier = pltpu.get_barrier_semaphore()

    def greet(step, _):
        pl.semaphore_signal(
            barrier, inc=1, device_id={"gz": lax.rem(me + step, n)},
            device_id_type=pl.DeviceIdType.MESH,
        )
        return 0

    lax.fori_loop(1, n, greet, 0)

    def lanes_of(rows):
        return lax.broadcasted_iota(jnp.int32, (rows, LANES), 1)

    xpad[:, 0:LANES] = jnp.zeros((240, LANES), BF16)
    xpad[:, cells + LANES : cells + 2 * LANES] = jnp.zeros((240, LANES), BF16)
    border = jnp.zeros((576, LANES), F32)
    shares[:, 0:LANES] = border
    shares[:, hcells // 2 + LANES : hcells // 2 + 2 * LANES] = border
    mpad[:, 0:LANES] = jnp.zeros((192, LANES), BF16)
    mpad[:, cells + LANES : cells + 2 * LANES] = jnp.zeros((192, LANES), BF16)

    def remote(src, dst, send, recv, target):
        return pltpu.make_async_remote_copy(
            src_ref=src, dst_ref=dst, send_sem=send, recv_sem=recv,
            device_id={"gz": target}, device_id_type=pl.DeviceIdType.MESH,
        )

    def exchange(to_left, at_right, to_right, at_left, send, recv, seg):
        go_left = remote(to_left, at_right, send.at[0, seg], recv.at[0, seg], left)
        go_right = remote(to_right, at_left, send.at[1, seg], recv.at[1, seg], right)

        def start():
            @pl.when(has_left)
            def _():
                go_left.start()

            @pl.when(has_right)
            def _():
                go_right.start()

        def receive():
            @pl.when(has_right)
            def _():
                go_left.wait_recv()

            @pl.when(has_left)
            def _():
                go_right.wait_recv()

            @pl.when(jnp.logical_not(has_right))
            def _():
                at_right[...] = jnp.zeros(at_right.shape, at_right.dtype)

            @pl.when(jnp.logical_not(has_left))
            def _():
                at_left[...] = jnp.zeros(at_left.shape, at_left.dtype)

        def sent():
            @pl.when(has_left)
            def _():
                go_left.wait_send()

            @pl.when(has_right)
            def _():
                go_right.wait_send()

        return start, receive, sent

    depth = 4
    f_rows = f_ref.shape[0]
    channels_in = f_rows // depth
    loads[0].wait()
    planes[...] = f_ref[...].reshape(f_rows * ny, LANES).astype(F32)
    rim_pad = jnp.zeros((16 - channels_in, LANES), F32)
    for y in range(ny):
        at = slice(y * LANES, (y + 1) * LANES)
        for side in range(2):
            rim = planes[pl.ds(side * (depth - 1) * ny + y, channels_in, stride=depth * ny), :]
            rim_ref[16 * side : 16 * side + 16, at] = jnp.concatenate(
                [rim, rim_pad], axis=0
            ).astype(BF16)

    pl.semaphore_wait(barrier, n - 1)

    features_start, features_receive, features_sent = exchange(
        rim_ref.at[0:16], fhalo.at[16:32], rim_ref.at[16:32], fhalo.at[0:16], fsend, frecv, 0
    )
    features_start()
    for load in loads[1:]:
        load.wait()

    nbx = LANES // BX
    count = tissue_ref.shape[1]
    blocks = (ny // BY) * nbx
    shape = (count, count)
    r = lax.broadcasted_iota(jnp.int32, shape, 0)
    c = lax.broadcasted_iota(jnp.int32, shape, 1)
    own_row = jnp.broadcast_to(owners_ref[...], shape)
    tis_row = jnp.broadcast_to(tissue_ref[...], shape)
    own_col = jnp.sum(jnp.where(r == c, own_row, 0), axis=1, keepdims=True)
    tis_col = jnp.sum(jnp.where(r == c, tis_row, 0), axis=1, keepdims=True)
    rank = jnp.sum(jnp.where((own_row == own_col) & (c < r), 1, 0), axis=1, keepdims=True)
    slot_col = own_col * SEND_CAP + rank
    wide_shape = (count, blocks * PART)
    block_of = lax.broadcasted_iota(jnp.int32, wide_shape, 1) // PART
    slot_row = (
        jnp.sum(jnp.where(tis_col == block_of, slot_col + 1, 0), axis=0, keepdims=True) - 1
    )
    group = 256

    def pick_rows(g, _):
        row = lax.broadcasted_iota(jnp.int32, (group, blocks * PART), 0) + g * group
        col = lax.broadcasted_iota(jnp.int32, (group, blocks * PART), 1)
        pick = (row // PART == slot_row) & (lax.rem(row, PART) == lax.rem(col, PART))
        picks[pl.ds(pl.multiple_of(g * group, group), group), :] = jnp.where(
            pick, 1.0, 0.0
        ).astype(BF16)
        return 0

    groups = n * SEND_CAP * PART // group
    lax.fori_loop(0, groups, pick_rows, 0)

    w2 = w2_ref[...].astype(F32)
    blank = jnp.zeros((96, 144), F32)
    for b in range(3):
        taps = [w2[:, 432 * a + 144 * b : 432 * a + 144 * b + 144] for a in range(3)]
        for z in range(2):
            w2_band[192 * b + 96 * z : 192 * b + 96 * z + 96, :] = jnp.concatenate(
                [blank] * z + taps + [blank] * (1 - z), axis=1
            ).astype(BF16)

    taps = w1_ref.shape[1]
    tap = lax.broadcasted_iota(jnp.int32, (1, taps), 1)
    w1 = w1_ref[...].astype(F32)
    by_y = jnp.concatenate(
        [jnp.where(lax.rem(tap // 36, 3) == b, w1, 0.0) for b in range(3)], axis=0
    ).astype(BF16)
    tap = lax.broadcasted_iota(jnp.int32, (taps, 1), 0)
    channel = lax.rem(tap, 12)
    x_off = lax.rem(tap // 12, 3)
    z_off = tap // 108
    target = lax.broadcasted_iota(jnp.int32, (taps, 240), 1)
    for z in range(depth):
        plane = z_off + (z - 1)
        row = jnp.where(
            plane < 0,
            channel,
            jnp.where(plane == depth, 64 + channel, 16 + depth * channel + plane),
        )
        place = jnp.where(target == x_off * 80 + row, 1.0, 0.0).astype(BF16)
        w1_band[144 * z : 144 * z + 144, :] = jnp.dot(
            by_y, place, preferred_element_type=F32
        ).astype(BF16)

    w3 = w3_ref[...].astype(F32)
    bands = []
    for bc in range(9):
        columns = jnp.concatenate(
            [w3[:, (9 * a + bc) * 48 : (9 * a + bc) * 48 + 48] for a in range(3)], axis=1
        )
        for zo in range(6):
            first = 48 * (zo - 2)
            low, high = max(first, 0), min(first + 144, 192)
            pieces = [columns[:, low - first : high - first]]
            if low > 0:
                pieces.insert(0, jnp.zeros((12, low), F32))
            if high < 192:
                pieces.append(jnp.zeros((12, 192 - high), F32))
            bands.append(jnp.concatenate(pieces, axis=1))
    w3_band[...] = jnp.concatenate(bands, axis=0).astype(BF16)

    def shift_rows(vf, row0, to):
        rows = vf.shape[0]
        lane = lanes_of(rows)
        xpad[row0 : row0 + rows, to] = lane_shift(vf, 1, lane).astype(BF16)
        xpad[80 + row0 : 80 + row0 + rows, to] = vf.astype(BF16)
        xpad[160 + row0 : 160 + row0 + rows, to] = lane_shift(vf, -1, lane).astype(BF16)

    for y in range(ny):
        shift_rows(
            planes[pl.ds(y, f_rows, stride=ny), :], 16, slice((y + 1) * LANES, (y + 2) * LANES)
        )
    features_receive()

    def shift_rims(y, _):
        at = pl.ds(pl.multiple_of(y * LANES, LANES), LANES)
        to = pl.ds(pl.multiple_of((y + 1) * LANES, LANES), LANES)
        shift_rows(fhalo[0:16, at].astype(F32), 0, to)
        shift_rows(fhalo[16:32, at].astype(F32), 64, to)
        return 0

    lax.fori_loop(0, ny, shift_rims, 0, unroll=4)

    half = LANES // 2

    def shift_pool(plane, v, to):
        at = lax.rem(lanes_of(48), half)
        before = jnp.where(at >= 1, pltpu.roll(v, 1, axis=1), 0.0)
        after = jnp.where(at < half - 1, pltpu.roll(v, LANES - 1, axis=1), 0.0)
        pool[144 * plane : 144 * plane + 48, to] = before.astype(BF16)
        pool[144 * plane + 96 : 144 * plane + 144, to] = after.astype(BF16)

    def sum_rows(product, offset, held):
        one = slice(0, LANES)
        two = slice(LANES, 2 * LANES)
        done = [
            held[0] + offset(product, 2, one),
            held[1] + offset(product, 1, one) + offset(product, 2, two),
        ]
        held[0] = offset(product, 0, one) + offset(product, 1, two)
        held[1] = offset(product, 0, two)
        return done

    def first_offset(product, b, at):
        return jnp.concatenate(
            [product[144 * z + 48 * b : 144 * z + 48 * b + 48, at] for z in range(depth)], axis=0
        )

    def first_product(pair):
        at = pl.ds(pl.multiple_of(pair * 2 * LANES, 2 * LANES), 2 * LANES)
        return jnp.dot(w1_band[...], xpad[:, at], preferred_element_type=F32)

    carry[...] = jnp.zeros(carry.shape, F32)
    sum_rows(first_product(0), first_offset, carry)

    def first_conv(i, _):
        base = pl.multiple_of(i * 2 * LANES, 2 * LANES)
        acc = jnp.concatenate(sum_rows(first_product(i + 1), first_offset, carry), axis=1)
        acc = jnp.maximum(acc, 0.0)
        fmap[:, pl.ds(base, 2 * LANES)] = acc.astype(BF16)
        deep = jnp.concatenate(
            [jnp.maximum(acc[0:48], acc[48:96]), jnp.maximum(acc[96:144], acc[144:192])], axis=0
        )
        wide = jnp.maximum(deep[:, 0:LANES], deep[:, LANES : 2 * LANES])
        both = jnp.maximum(wide, pltpu.roll(wide, LANES - 1, axis=1))
        rows_max[:, pl.ds(pl.multiple_of(i * LANES, LANES), LANES)] = both.astype(BF16)
        return 0

    compact = jnp.where(
        lax.broadcasted_iota(jnp.int32, (2 * LANES, LANES), 0)
        == 2 * lax.broadcasted_iota(jnp.int32, (2 * LANES, LANES), 1),
        1.0,
        0.0,
    ).astype(BF16)
    double = jnp.where(
        lax.broadcasted_iota(jnp.int32, (LANES, 2 * LANES), 0)
        == lax.broadcasted_iota(jnp.int32, (LANES, 2 * LANES), 1) // 2,
        1.0,
        0.0,
    ).astype(BF16)

    seg_rows = hy // SEGS

    def pooled(seg):
        at = pl.ds(pl.multiple_of(seg * 2 * LANES, 2 * LANES), 2 * LANES)
        return exchange(
            pool.at[192:240, at], pool.at[480:528, at],
            pool.at[336:384, at], pool.at[48:96, at], psend, precv, seg,
        )

    def tile_at(tile):
        return pl.ds(pl.multiple_of(tile * LANES, LANES), LANES)

    def first_segment(seg, _):
        lax.fori_loop(
            0, seg_rows, lambda i, _: first_conv(seg * seg_rows + i, 0), 0, unroll=True
        )
        pairs = [
            rows_max[:, pl.ds(pl.multiple_of((2 * seg + t) * 2 * LANES, 2 * LANES), 2 * LANES)]
            for t in range(2)
        ]
        packed = jnp.dot(jnp.concatenate(pairs, axis=0), compact, preferred_element_type=F32)
        for t in range(2):
            for z in range(2):
                pool[144 * z + 192 : 144 * z + 240, tile_at(2 * seg + t)] = packed[
                    96 * t + 48 * z : 96 * t + 48 * z + 48
                ].astype(BF16)
        pooled(seg)[0]()
        for t in range(2):
            for z in range(2):
                shift_pool(
                    z + 1, packed[96 * t + 48 * z : 96 * t + 48 * z + 48], tile_at(2 * seg + t)
                )
        return 0

    lax.fori_loop(0, SEGS, first_segment, 0)

    def second_segment(seg, _):
        pooled(seg)[1]()
        for t in range(2):
            to = tile_at(2 * seg + t)
            shift_pool(0, pool[48:96, to].astype(F32), to)
            shift_pool(3, pool[480:528, to].astype(F32), to)
        at = pl.ds(pl.multiple_of(seg * 2 * LANES, 2 * LANES), 2 * LANES)
        to = pl.ds(pl.multiple_of((2 * seg + 1) * LANES, LANES), 2 * LANES)
        shares[:, to] = jnp.dot(w2_band[...], pool[:, at], preferred_element_type=F32)
        return 0

    lax.fori_loop(0, SEGS, second_segment, 0)

    def second_conv(i, _):
        lower = lanes_of(192) < half

        def turned(row0, tile):
            return pltpu.roll(shares[row0 : row0 + 192, tile_at(tile)], half, axis=1)

        acc = (
            shares[192:384, tile_at(i + 1)]
            + jnp.where(lower, turned(0, i), turned(0, i + 1))
            + jnp.where(lower, turned(384, i + 1), turned(384, i + 2))
        )
        second = jnp.maximum(acc, 0.0).astype(BF16)
        second = jnp.dot(second, double, preferred_element_type=F32).astype(BF16)
        for side in range(2):
            lifted = jnp.dot(
                wl_ref[...], second[96 * side : 96 * side + 96], preferred_element_type=F32
            )
            for row in range(4):
                part = lifted[:, (row // 2) * LANES : (row // 2 + 1) * LANES]
                for deep in range(2):
                    plane = 48 * (2 * side + deep)
                    own = fmap[plane : plane + 48, tile_at(i * 4 + row)]
                    mpad[plane : plane + 48, tile_at(i * 4 + row + 1)] = (
                        part + own.astype(F32)
                    ).astype(BF16)
        return 0

    lax.fori_loop(0, hy // 2, second_conv, 0, unroll=4)

    def third_offset(product, b, at):
        return product[216 * b : 216 * b + 216, at]

    def third_product(pair):
        at = pl.ds(pl.multiple_of(pair * 2 * LANES, 2 * LANES), 2 * LANES)
        return jnp.dot(w3_band[...], mpad[:, at], preferred_element_type=F32)

    carry3[...] = jnp.zeros(carry3.shape, F32)
    sum_rows(third_product(0), third_offset, carry3)

    def third_conv(i, _):
        base = pl.multiple_of(i * 2 * LANES, 2 * LANES)
        done = sum_rows(third_product(i + 1), third_offset, carry3)
        lane = lanes_of(72)
        for row in range(2):
            acc = done[row]
            total = (
                acc[72:144] + lane_shift(acc[0:72], 1, lane) + lane_shift(acc[144:216], -1, lane)
            )
            to = pl.ds(pl.multiple_of(base + row * LANES, LANES), LANES)
            terms[:, to] = total
            edge[0:16, to] = total[0:16].astype(BF16)
            edge[16:32, to] = total[56:72].astype(BF16)
        return 0

    def edges(seg):
        at = pl.ds(pl.multiple_of(seg * BY * LANES, BY * LANES), BY * LANES)
        return exchange(
            edge.at[0:16, at], ehalo.at[16:32, at],
            edge.at[16:32, at], ehalo.at[0:16, at], esend, erecv, seg,
        )

    def third_segment(seg, _):
        lax.fori_loop(
            0, BY // 2, lambda i, _: third_conv(seg * (BY // 2) + i, 0), 0, unroll=True
        )
        edges(seg)[0]()
        return 0

    lax.fori_loop(0, ny // BY, third_segment, 0)

    spread_row = lax.broadcasted_iota(jnp.int32, (BY * LANES, LANES), 0)
    spread_col = lax.broadcasted_iota(jnp.int32, (BY * LANES, LANES), 1)
    spread = jnp.where(
        spread_col == (spread_row // LANES) * BX + lax.rem(spread_row, BX), 1.0, 0.0
    ).astype(BF16)
    block_mask = (
        lax.broadcasted_iota(jnp.int32, (nbx * PART, LANES), 0) // PART
        == lax.broadcasted_iota(jnp.int32, (nbx * PART, LANES), 1) // BX
    )
    directions, channels = wa_ref.shape

    def head_matrix(rows, first_at, second_at):
        across = 3 * rows
        inside = lax.rem(lax.broadcasted_iota(jnp.int32, (channels, across), 1), rows)
        channel = lax.broadcasted_iota(jnp.int32, (channels, across), 0)
        hit = (inside == channel + first_at) | (inside == channel + second_at)
        columns = jnp.dot(
            wa_ref[...], jnp.where(hit, 1.0, 0.0).astype(BF16), preferred_element_type=F32
        ).astype(BF16)
        turn = lax.broadcasted_iota(jnp.int32, (PART, directions), 0) // 2
        turn = turn == lax.broadcasted_iota(jnp.int32, (PART, directions), 1)
        full = jnp.dot(
            jnp.where(turn, 1.0, 0.0).astype(BF16), columns, preferred_element_type=F32
        )
        at = lax.rem(lax.broadcasted_iota(jnp.int32, (PART, across), 1), rows)
        odd = lax.rem(lax.broadcasted_iota(jnp.int32, (PART, across), 0), 2) == 1
        start = jnp.where(odd, second_at, first_at)
        keep = (at >= start) & (at < start + channels)
        return jnp.where(keep, full, 0.0).astype(BF16)

    def head_rows(matrix, total_of):
        def head(by, _):
            parts = []
            for pair in range(BY // 2):
                at = pl.ds(pl.multiple_of((by * BY + 2 * pair) * LANES, LANES), 2 * LANES)
                third = jnp.maximum(total_of(at), 0.0)
                one = third.astype(BF16).astype(F32)
                rest = third - one
                two = rest.astype(BF16).astype(F32)
                three = rest - two
                split = jnp.concatenate([one, two, three], axis=0).astype(BF16)
                logits = jnp.dot(matrix, split, preferred_element_type=F32)
                affinity = 1.0 / (1.0 + jnp.exp(-logits))
                for row in range(2):
                    tile = affinity[:, row * LANES : (row + 1) * LANES]
                    stacked = jnp.concatenate([tile] * nbx, axis=0)
                    parts.append(jnp.where(block_mask, stacked, 0.0).astype(BF16))
            rows = nbx * PART
            masked[pl.ds(pl.multiple_of(by * rows, rows), rows), :] = jnp.concatenate(
                parts, axis=1
            )
            return 0

        return head

    per = SEND_CAP * PART

    def message(part, step):
        target = lax.rem(me + step, n)
        return remote(
            outgoing.at[part, pl.ds(pl.multiple_of(target * per, per), per)],
            landing.at[part, me], asend.at[part, step], arecv.at[part, step], target,
        )

    def send_part(part):
        tiles[part] = jnp.dot(masked[...], spread, preferred_element_type=F32).astype(BF16)

        def route(g, _):
            at = pl.ds(pl.multiple_of(g * group, group), group)
            outgoing[part, at, :] = jnp.dot(
                picks[at, :], tiles[part], preferred_element_type=F32
            ).astype(BF16)
            return 0

        def send(step, _):
            message(part, step).start()
            return 0

        lax.fori_loop(0, groups, route, 0)
        lax.fori_loop(1, n, send, 0)
        landing[part, me] = outgoing[part, pl.ds(pl.multiple_of(me * per, per), per), :]

    inner_head = head_rows(head_matrix(24, 0, 12), lambda at: terms[24:48, at])
    lax.fori_loop(0, ny // BY, inner_head, 0, unroll=2)
    send_part(0)

    def outer_total(at):
        low = terms[8:24, at] + ehalo[0:16, at].astype(F32)
        high = terms[48:64, at] + ehalo[16:32, at].astype(F32)
        return jnp.concatenate([low, high], axis=0)

    outer_head = head_rows(head_matrix(32, 4, 16), outer_total)

    def outer_segment(by, _):
        edges(by)[1]()
        return outer_head(by, 0)

    lax.fori_loop(0, ny // BY, outer_segment, 0)
    send_part(1)

    features_sent()

    def pooled_sent(seg, _):
        pooled(seg)[2]()
        return 0

    def edges_sent(seg, _):
        edges(seg)[2]()
        return 0

    lax.fori_loop(0, SEGS, pooled_sent, 0)
    lax.fori_loop(0, ny // BY, edges_sent, 0)

    def receive(step, _):
        message(0, step).wait()
        message(1, step).wait()
        return 0

    lax.fori_loop(1, n, receive, 0)

    slots = n * SEND_CAP
    used = 2 * directions
    line = lax.broadcasted_iota(jnp.int32, (used * slots, slots * PART), 0)
    source = lax.rem(line, slots) * PART + line // slots
    gather = jnp.where(
        source == lax.broadcasted_iota(jnp.int32, (used * slots, slots * PART), 1), 1.0, 0.0
    ).astype(BF16)
    inner_rows, outer_rows = [
        jnp.dot(
            gather, landing[part].reshape(slots * PART, LANES), preferred_element_type=F32
        )
        for part in range(2)
    ]
    lines = []
    for d in range(directions):
        for rows_of, turn in ((outer_rows, 0), (inner_rows, 0), (inner_rows, 1), (outer_rows, 1)):
            k = (2 * d + turn) * slots
            lines.append(rows_of[k : k + slots])
    whole = jnp.concatenate(lines, axis=1)
    for s in range(n):
        out_ref[s] = whole[SEND_CAP * s : SEND_CAP * s + SEND_CAP].astype(BF16)


def on_device(features, w_first, w_second, w_lift, w_merge, w_affine, tissue, owners):
    n = lax.axis_size("gz")
    channels, depth, ny, nx = features.shape
    cells = ny * nx
    hcells = (ny // 2) * nx
    flat = features.reshape(channels * depth, ny, nx)
    operands = (flat, w_first, w_second, w_lift, w_merge, w_affine, tissue, owners)
    per = SEND_CAP * PART
    blocks = (ny // BY) * (nx // BX)
    vmem = pl.BlockSpec(memory_space=pltpu.VMEM)
    routed = pl.pallas_call(
        functools.partial(kernel, n, ny),
        out_shape=jax.ShapeDtypeStruct((n, SEND_CAP, w_affine.shape[0] * depth * LANES), BF16),
        in_specs=[pl.BlockSpec(memory_space=pltpu.HBM)] * len(operands),
        out_specs=vmem,
        scratch_shapes=[
            *[pltpu.VMEM(operand.shape, operand.dtype) for operand in operands],
            pltpu.SemaphoreType.DMA((len(operands),)),
            pltpu.VMEM((channels * depth * ny, LANES), F32),
            pltpu.VMEM((32, cells), BF16),
            pltpu.VMEM((576, 240), BF16),
            pltpu.VMEM((2, 192, LANES), F32),
            pltpu.VMEM((2, 216, LANES), F32),
            pltpu.VMEM((2, n, per, LANES), BF16),
            pltpu.VMEM((32, cells), BF16),
            pltpu.VMEM((240, cells + 2 * LANES), BF16),
            pltpu.VMEM((192, cells), BF16),
            pltpu.VMEM((96, hcells), BF16),
            pltpu.VMEM((576, hcells // 2), BF16),
            pltpu.VMEM((576, hcells // 2 + 2 * LANES), F32),
            pltpu.VMEM((192, cells + 2 * LANES), BF16),
            pltpu.VMEM((72, cells), F32),
            pltpu.VMEM((32, cells), BF16),
            pltpu.VMEM((32, cells), BF16),
            pltpu.VMEM((576, 576), BF16),
            pltpu.VMEM((648, 192), BF16),
            pltpu.VMEM((n * per, blocks * PART), BF16),
            pltpu.VMEM((blocks * PART, BY * LANES), BF16),
            pltpu.VMEM((2, blocks * PART, LANES), BF16),
            pltpu.VMEM((2, n * per, LANES), BF16),
            pltpu.SemaphoreType.DMA((2, 1)),
            pltpu.SemaphoreType.DMA((2, 1)),
            pltpu.SemaphoreType.DMA((2, SEGS)),
            pltpu.SemaphoreType.DMA((2, SEGS)),
            pltpu.SemaphoreType.DMA((2, ny // BY)),
            pltpu.SemaphoreType.DMA((2, ny // BY)),
            pltpu.SemaphoreType.DMA((2, n)),
            pltpu.SemaphoreType.DMA((2, n)),
        ],
        compiler_params=pltpu.CompilerParams(
            collective_id=0, has_side_effects=True, vmem_limit_bytes=63 * 1024 * 1024
        ),
        cost_estimate=pl.CostEstimate(
            flops=1600000000, bytes_accessed=2000000, transcendentals=65536
        ),
    )(*operands)
    return routed[None]


def solution(mesh):
    placed = (
        P(None, ("grp", "gz"), None, None),
        P(),
        P(),
        P(),
        P(),
        P(),
        P(("grp", "gz"), None),
        P(("grp", "gz"), None),
    )
    return jax.shard_map(
        on_device,
        mesh=mesh,
        in_specs=placed,
        out_specs=P(("grp", "gz"), None, None, None),
        check_vma=False,
    )
```

```python
import functools

import jax
import jax.numpy as jnp
from jax import lax
from jax.experimental import pallas as pl
from jax.experimental.pallas import tpu as pltpu
from jax.sharding import PartitionSpec as P

BY = 8
BX = 16
SEND_CAP = 2
LANES = 128
PART = 8
SEGS = 4
F32 = jnp.float32
BF16 = jnp.bfloat16


def lane_shift(tile, step, lane):
    rolled = pltpu.roll(tile, step % LANES, axis=1)
    keep = lane >= step if step > 0 else lane < LANES + step
    return jnp.where(keep, rolled, 0.0)


def kernel(
    n, ny,
    f_ref, w1_ref, w2_ref, wl_ref, w3_ref, wa_ref, tissue_ref, owners_ref,
    out_ref,
    planes,
    rim_ref, w1_band, carry, carry3, landing, fhalo, xpad, fmap, rows_max, pool, shares, mpad, terms, edge, ehalo, w2_band, w3_band, picks, masked, tiles, outgoing,
    fsend, frecv, psend, precv, esend, erecv, asend, arecv,
):
    me = lax.axis_index("gz")
    has_left = me > 0
    has_right = me < n - 1
    left = me - 1
    right = me + 1
    cells = ny * LANES
    hy = ny // 2
    hcells = hy * LANES

    barrier = pltpu.get_barrier_semaphore()

    def greet(step, _):
        pl.semaphore_signal(
            barrier, inc=1, device_id={"gz": lax.rem(me + step, n)},
            device_id_type=pl.DeviceIdType.MESH,
        )
        return 0

    lax.fori_loop(1, n, greet, 0)

    def lanes_of(rows):
        return lax.broadcasted_iota(jnp.int32, (rows, LANES), 1)

    xpad[:, 0:LANES] = jnp.zeros((240, LANES), BF16)
    xpad[:, cells + LANES : cells + 2 * LANES] = jnp.zeros((240, LANES), BF16)
    border = jnp.zeros((576, LANES), F32)
    shares[:, 0:LANES] = border
    shares[:, hcells // 2 + LANES : hcells // 2 + 2 * LANES] = border
    mpad[:, 0:LANES] = jnp.zeros((192, LANES), BF16)
    mpad[:, cells + LANES : cells + 2 * LANES] = jnp.zeros((192, LANES), BF16)

    def remote(src, dst, send, recv, target):
        return pltpu.make_async_remote_copy(
            src_ref=src, dst_ref=dst, send_sem=send, recv_sem=recv,
            device_id={"gz": target}, device_id_type=pl.DeviceIdType.MESH,
        )

    def exchange(to_left, at_right, to_right, at_left, send, recv, seg):
        go_left = remote(to_left, at_right, send.at[0, seg], recv.at[0, seg], left)
        go_right = remote(to_right, at_left, send.at[1, seg], recv.at[1, seg], right)

        def start():
            @pl.when(has_left)
            def _():
                go_left.start()

            @pl.when(has_right)
            def _():
                go_right.start()

        def receive():
            @pl.when(has_right)
            def _():
                go_left.wait_recv()

            @pl.when(has_left)
            def _():
                go_right.wait_recv()

            @pl.when(jnp.logical_not(has_right))
            def _():
                at_right[...] = jnp.zeros(at_right.shape, at_right.dtype)

            @pl.when(jnp.logical_not(has_left))
            def _():
                at_left[...] = jnp.zeros(at_left.shape, at_left.dtype)

        def sent():
            @pl.when(has_left)
            def _():
                go_left.wait_send()

            @pl.when(has_right)
            def _():
                go_right.wait_send()

        return start, receive, sent

    depth = 4
    f_rows = f_ref.shape[0]
    channels_in = f_rows // depth
    planes[...] = f_ref[...].reshape(f_rows * ny, LANES).astype(F32)
    rim_pad = jnp.zeros((16 - channels_in, LANES), F32)
    for y in range(ny):
        at = slice(y * LANES, (y + 1) * LANES)
        for side in range(2):
            rim = planes[pl.ds(side * (depth - 1) * ny + y, channels_in, stride=depth * ny), :]
            rim_ref[16 * side : 16 * side + 16, at] = jnp.concatenate(
                [rim, rim_pad], axis=0
            ).astype(BF16)

    pl.semaphore_wait(barrier, n - 1)

    features_start, features_receive, features_sent = exchange(
        rim_ref.at[0:16], fhalo.at[16:32], rim_ref.at[16:32], fhalo.at[0:16], fsend, frecv, 0
    )
    features_start()
    nbx = LANES // BX
    count = tissue_ref.shape[1]
    blocks = (ny // BY) * nbx
    shape = (count, count)
    r = lax.broadcasted_iota(jnp.int32, shape, 0)
    c = lax.broadcasted_iota(jnp.int32, shape, 1)
    own_row = jnp.broadcast_to(owners_ref[...], shape)
    tis_row = jnp.broadcast_to(tissue_ref[...], shape)
    own_col = jnp.sum(jnp.where(r == c, own_row, 0), axis=1, keepdims=True)
    tis_col = jnp.sum(jnp.where(r == c, tis_row, 0), axis=1, keepdims=True)
    rank = jnp.sum(jnp.where((own_row == own_col) & (c < r), 1, 0), axis=1, keepdims=True)
    slot_col = own_col * SEND_CAP + rank
    wide_shape = (count, blocks * PART)
    block_of = lax.broadcasted_iota(jnp.int32, wide_shape, 1) // PART
    slot_row = (
        jnp.sum(jnp.where(tis_col == block_of, slot_col + 1, 0), axis=0, keepdims=True) - 1
    )
    group = 256

    def pick_rows(g, _):
        row = lax.broadcasted_iota(jnp.int32, (group, blocks * PART), 0) + g * group
        col = lax.broadcasted_iota(jnp.int32, (group, blocks * PART), 1)
        pick = (row // PART == slot_row) & (lax.rem(row, PART) == lax.rem(col, PART))
        picks[pl.ds(pl.multiple_of(g * group, group), group), :] = jnp.where(
            pick, 1.0, 0.0
        ).astype(BF16)
        return 0

    groups = n * SEND_CAP * PART // group
    lax.fori_loop(0, groups, pick_rows, 0)

    w2 = w2_ref[...].astype(F32)
    blank = jnp.zeros((96, 144), F32)
    for b in range(3):
        taps = [w2[:, 432 * a + 144 * b : 432 * a + 144 * b + 144] for a in range(3)]
        for z in range(2):
            w2_band[192 * b + 96 * z : 192 * b + 96 * z + 96, :] = jnp.concatenate(
                [blank] * z + taps + [blank] * (1 - z), axis=1
            ).astype(BF16)

    taps = w1_ref.shape[1]
    tap = lax.broadcasted_iota(jnp.int32, (1, taps), 1)
    w1 = w1_ref[...].astype(F32)
    by_y = jnp.concatenate(
        [jnp.where(lax.rem(tap // 36, 3) == b, w1, 0.0) for b in range(3)], axis=0
    ).astype(BF16)
    tap = lax.broadcasted_iota(jnp.int32, (taps, 1), 0)
    channel = lax.rem(tap, 12)
    x_off = lax.rem(tap // 12, 3)
    z_off = tap // 108
    target = lax.broadcasted_iota(jnp.int32, (taps, 240), 1)
    for z in range(depth):
        plane = z_off + (z - 1)
        row = jnp.where(
            plane < 0,
            channel,
            jnp.where(plane == depth, 64 + channel, 16 + depth * channel + plane),
        )
        place = jnp.where(target == x_off * 80 + row, 1.0, 0.0).astype(BF16)
        w1_band[144 * z : 144 * z + 144, :] = jnp.dot(
            by_y, place, preferred_element_type=F32
        ).astype(BF16)

    w3 = w3_ref[...].astype(F32)
    bands = []
    for bc in range(9):
        columns = jnp.concatenate(
            [w3[:, (9 * a + bc) * 48 : (9 * a + bc) * 48 + 48] for a in range(3)], axis=1
        )
        for zo in range(6):
            first = 48 * (zo - 2)
            low, high = max(first, 0), min(first + 144, 192)
            pieces = [columns[:, low - first : high - first]]
            if low > 0:
                pieces.insert(0, jnp.zeros((12, low), F32))
            if high < 192:
                pieces.append(jnp.zeros((12, 192 - high), F32))
            bands.append(jnp.concatenate(pieces, axis=1))
    w3_band[...] = jnp.concatenate(bands, axis=0).astype(BF16)

    def shift_rows(vf, row0, to):
        rows = vf.shape[0]
        lane = lanes_of(rows)
        xpad[row0 : row0 + rows, to] = lane_shift(vf, 1, lane).astype(BF16)
        xpad[80 + row0 : 80 + row0 + rows, to] = vf.astype(BF16)
        xpad[160 + row0 : 160 + row0 + rows, to] = lane_shift(vf, -1, lane).astype(BF16)

    for y in range(ny):
        shift_rows(
            planes[pl.ds(y, f_rows, stride=ny), :], 16, slice((y + 1) * LANES, (y + 2) * LANES)
        )
    features_receive()

    def shift_rims(y, _):
        at = pl.ds(pl.multiple_of(y * LANES, LANES), LANES)
        to = pl.ds(pl.multiple_of((y + 1) * LANES, LANES), LANES)
        shift_rows(fhalo[0:16, at].astype(F32), 0, to)
        shift_rows(fhalo[16:32, at].astype(F32), 64, to)
        return 0

    lax.fori_loop(0, ny, shift_rims, 0, unroll=4)

    half = LANES // 2

    def shift_pool(plane, v, to):
        at = lax.rem(lanes_of(48), half)
        before = jnp.where(at >= 1, pltpu.roll(v, 1, axis=1), 0.0)
        after = jnp.where(at < half - 1, pltpu.roll(v, LANES - 1, axis=1), 0.0)
        pool[144 * plane : 144 * plane + 48, to] = before.astype(BF16)
        pool[144 * plane + 96 : 144 * plane + 144, to] = after.astype(BF16)

    def sum_rows(product, offset, held):
        one = slice(0, LANES)
        two = slice(LANES, 2 * LANES)
        done = [
            held[0] + offset(product, 2, one),
            held[1] + offset(product, 1, one) + offset(product, 2, two),
        ]
        held[0] = offset(product, 0, one) + offset(product, 1, two)
        held[1] = offset(product, 0, two)
        return done

    def first_offset(product, b, at):
        return jnp.concatenate(
            [product[144 * z + 48 * b : 144 * z + 48 * b + 48, at] for z in range(depth)], axis=0
        )

    def first_product(pair):
        at = pl.ds(pl.multiple_of(pair * 2 * LANES, 2 * LANES), 2 * LANES)
        return jnp.dot(w1_band[...], xpad[:, at], preferred_element_type=F32)

    carry[...] = jnp.zeros(carry.shape, F32)
    sum_rows(first_product(0), first_offset, carry)

    def first_conv(i, _):
        base = pl.multiple_of(i * 2 * LANES, 2 * LANES)
        acc = jnp.concatenate(sum_rows(first_product(i + 1), first_offset, carry), axis=1)
        acc = jnp.maximum(acc, 0.0)
        fmap[:, pl.ds(base, 2 * LANES)] = acc.astype(BF16)
        deep = jnp.concatenate(
            [jnp.maximum(acc[0:48], acc[48:96]), jnp.maximum(acc[96:144], acc[144:192])], axis=0
        )
        wide = jnp.maximum(deep[:, 0:LANES], deep[:, LANES : 2 * LANES])
        both = jnp.maximum(wide, pltpu.roll(wide, LANES - 1, axis=1))
        rows_max[:, pl.ds(pl.multiple_of(i * LANES, LANES), LANES)] = both.astype(BF16)
        return 0

    compact = jnp.where(
        lax.broadcasted_iota(jnp.int32, (2 * LANES, LANES), 0)
        == 2 * lax.broadcasted_iota(jnp.int32, (2 * LANES, LANES), 1),
        1.0,
        0.0,
    ).astype(BF16)
    double = jnp.where(
        lax.broadcasted_iota(jnp.int32, (LANES, 2 * LANES), 0)
        == lax.broadcasted_iota(jnp.int32, (LANES, 2 * LANES), 1) // 2,
        1.0,
        0.0,
    ).astype(BF16)

    seg_rows = hy // SEGS

    def pooled(seg):
        at = pl.ds(pl.multiple_of(seg * 2 * LANES, 2 * LANES), 2 * LANES)
        return exchange(
            pool.at[192:240, at], pool.at[480:528, at],
            pool.at[336:384, at], pool.at[48:96, at], psend, precv, seg,
        )

    def tile_at(tile):
        return pl.ds(pl.multiple_of(tile * LANES, LANES), LANES)

    def first_segment(seg, _):
        lax.fori_loop(
            0, seg_rows, lambda i, _: first_conv(seg * seg_rows + i, 0), 0, unroll=True
        )
        pairs = [
            rows_max[:, pl.ds(pl.multiple_of((2 * seg + t) * 2 * LANES, 2 * LANES), 2 * LANES)]
            for t in range(2)
        ]
        packed = jnp.dot(jnp.concatenate(pairs, axis=0), compact, preferred_element_type=F32)
        for t in range(2):
            for z in range(2):
                pool[144 * z + 192 : 144 * z + 240, tile_at(2 * seg + t)] = packed[
                    96 * t + 48 * z : 96 * t + 48 * z + 48
                ].astype(BF16)
        pooled(seg)[0]()
        for t in range(2):
            for z in range(2):
                shift_pool(
                    z + 1, packed[96 * t + 48 * z : 96 * t + 48 * z + 48], tile_at(2 * seg + t)
                )
        return 0

    lax.fori_loop(0, SEGS, first_segment, 0)

    def second_segment(seg, _):
        pooled(seg)[1]()
        for t in range(2):
            to = tile_at(2 * seg + t)
            shift_pool(0, pool[48:96, to].astype(F32), to)
            shift_pool(3, pool[480:528, to].astype(F32), to)
        at = pl.ds(pl.multiple_of(seg * 2 * LANES, 2 * LANES), 2 * LANES)
        to = pl.ds(pl.multiple_of((2 * seg + 1) * LANES, LANES), 2 * LANES)
        shares[:, to] = jnp.dot(w2_band[...], pool[:, at], preferred_element_type=F32)
        return 0

    lax.fori_loop(0, SEGS, second_segment, 0)

    def second_conv(i, _):
        lower = lanes_of(192) < half

        def turned(row0, tile):
            return pltpu.roll(shares[row0 : row0 + 192, tile_at(tile)], half, axis=1)

        acc = (
            shares[192:384, tile_at(i + 1)]
            + jnp.where(lower, turned(0, i), turned(0, i + 1))
            + jnp.where(lower, turned(384, i + 1), turned(384, i + 2))
        )
        second = jnp.maximum(acc, 0.0).astype(BF16)
        second = jnp.dot(second, double, preferred_element_type=F32).astype(BF16)
        for side in range(2):
            lifted = jnp.dot(
                wl_ref[...], second[96 * side : 96 * side + 96], preferred_element_type=F32
            )
            for row in range(4):
                part = lifted[:, (row // 2) * LANES : (row // 2 + 1) * LANES]
                for deep in range(2):
                    plane = 48 * (2 * side + deep)
                    own = fmap[plane : plane + 48, tile_at(i * 4 + row)]
                    mpad[plane : plane + 48, tile_at(i * 4 + row + 1)] = (
                        part + own.astype(F32)
                    ).astype(BF16)
        return 0

    lax.fori_loop(0, hy // 2, second_conv, 0, unroll=4)

    def third_offset(product, b, at):
        return product[216 * b : 216 * b + 216, at]

    def third_product(pair):
        at = pl.ds(pl.multiple_of(pair * 2 * LANES, 2 * LANES), 2 * LANES)
        return jnp.dot(w3_band[...], mpad[:, at], preferred_element_type=F32)

    carry3[...] = jnp.zeros(carry3.shape, F32)
    sum_rows(third_product(0), third_offset, carry3)

    def third_conv(i, _):
        base = pl.multiple_of(i * 2 * LANES, 2 * LANES)
        done = sum_rows(third_product(i + 1), third_offset, carry3)
        lane = lanes_of(72)
        for row in range(2):
            acc = done[row]
            total = (
                acc[72:144] + lane_shift(acc[0:72], 1, lane) + lane_shift(acc[144:216], -1, lane)
            )
            to = pl.ds(pl.multiple_of(base + row * LANES, LANES), LANES)
            terms[:, to] = total
            edge[0:16, to] = total[0:16].astype(BF16)
            edge[16:32, to] = total[56:72].astype(BF16)
        return 0

    def edges(seg):
        at = pl.ds(pl.multiple_of(seg * BY * LANES, BY * LANES), BY * LANES)
        return exchange(
            edge.at[0:16, at], ehalo.at[16:32, at],
            edge.at[16:32, at], ehalo.at[0:16, at], esend, erecv, seg,
        )

    def third_segment(seg, _):
        lax.fori_loop(
            0, BY // 2, lambda i, _: third_conv(seg * (BY // 2) + i, 0), 0, unroll=True
        )
        edges(seg)[0]()
        return 0

    lax.fori_loop(0, ny // BY, third_segment, 0)

    spread_row = lax.broadcasted_iota(jnp.int32, (BY * LANES, LANES), 0)
    spread_col = lax.broadcasted_iota(jnp.int32, (BY * LANES, LANES), 1)
    spread = jnp.where(
        spread_col == (spread_row // LANES) * BX + lax.rem(spread_row, BX), 1.0, 0.0
    ).astype(BF16)
    block_mask = (
        lax.broadcasted_iota(jnp.int32, (nbx * PART, LANES), 0) // PART
        == lax.broadcasted_iota(jnp.int32, (nbx * PART, LANES), 1) // BX
    )
    directions, channels = wa_ref.shape

    def head_matrix(rows, first_at, second_at):
        across = 3 * rows
        inside = lax.rem(lax.broadcasted_iota(jnp.int32, (channels, across), 1), rows)
        channel = lax.broadcasted_iota(jnp.int32, (channels, across), 0)
        hit = (inside == channel + first_at) | (inside == channel + second_at)
        columns = jnp.dot(
            wa_ref[...], jnp.where(hit, 1.0, 0.0).astype(BF16), preferred_element_type=F32
        ).astype(BF16)
        turn = lax.broadcasted_iota(jnp.int32, (PART, directions), 0) // 2
        turn = turn == lax.broadcasted_iota(jnp.int32, (PART, directions), 1)
        full = jnp.dot(
            jnp.where(turn, 1.0, 0.0).astype(BF16), columns, preferred_element_type=F32
        )
        at = lax.rem(lax.broadcasted_iota(jnp.int32, (PART, across), 1), rows)
        odd = lax.rem(lax.broadcasted_iota(jnp.int32, (PART, across), 0), 2) == 1
        start = jnp.where(odd, second_at, first_at)
        keep = (at >= start) & (at < start + channels)
        return jnp.where(keep, full, 0.0).astype(BF16)

    def head_rows(matrix, total_of):
        def head(by, _):
            parts = []
            for pair in range(BY // 2):
                at = pl.ds(pl.multiple_of((by * BY + 2 * pair) * LANES, LANES), 2 * LANES)
                third = jnp.maximum(total_of(at), 0.0)
                one = third.astype(BF16).astype(F32)
                rest = third - one
                two = rest.astype(BF16).astype(F32)
                three = rest - two
                split = jnp.concatenate([one, two, three], axis=0).astype(BF16)
                logits = jnp.dot(matrix, split, preferred_element_type=F32)
                affinity = 1.0 / (1.0 + jnp.exp(-logits))
                for row in range(2):
                    tile = affinity[:, row * LANES : (row + 1) * LANES]
                    stacked = jnp.concatenate([tile] * nbx, axis=0)
                    parts.append(jnp.where(block_mask, stacked, 0.0).astype(BF16))
            rows = nbx * PART
            masked[pl.ds(pl.multiple_of(by * rows, rows), rows), :] = jnp.concatenate(
                parts, axis=1
            )
            return 0

        return head

    per = SEND_CAP * PART

    def message(part, step):
        target = lax.rem(me + step, n)
        return remote(
            outgoing.at[part, pl.ds(pl.multiple_of(target * per, per), per)],
            landing.at[part, me], asend.at[part, step], arecv.at[part, step], target,
        )

    def send_part(part):
        tiles[part] = jnp.dot(masked[...], spread, preferred_element_type=F32).astype(BF16)

        def route(g, _):
            at = pl.ds(pl.multiple_of(g * group, group), group)
            outgoing[part, at, :] = jnp.dot(
                picks[at, :], tiles[part], preferred_element_type=F32
            ).astype(BF16)
            return 0

        def send(step, _):
            message(part, step).start()
            return 0

        lax.fori_loop(0, groups, route, 0)
        lax.fori_loop(1, n, send, 0)
        landing[part, me] = outgoing[part, pl.ds(pl.multiple_of(me * per, per), per), :]

    inner_head = head_rows(head_matrix(24, 0, 12), lambda at: terms[24:48, at])
    lax.fori_loop(0, ny // BY, inner_head, 0, unroll=2)
    send_part(0)

    def outer_total(at):
        low = terms[8:24, at] + ehalo[0:16, at].astype(F32)
        high = terms[48:64, at] + ehalo[16:32, at].astype(F32)
        return jnp.concatenate([low, high], axis=0)

    outer_head = head_rows(head_matrix(32, 4, 16), outer_total)

    def outer_segment(by, _):
        edges(by)[1]()
        return outer_head(by, 0)

    lax.fori_loop(0, ny // BY, outer_segment, 0)
    send_part(1)

    features_sent()

    def pooled_sent(seg, _):
        pooled(seg)[2]()
        return 0

    def edges_sent(seg, _):
        edges(seg)[2]()
        return 0

    lax.fori_loop(0, SEGS, pooled_sent, 0)
    lax.fori_loop(0, ny // BY, edges_sent, 0)

    def receive(step, _):
        message(0, step).wait()
        message(1, step).wait()
        return 0

    lax.fori_loop(1, n, receive, 0)

    slots = n * SEND_CAP
    used = 2 * directions
    line = lax.broadcasted_iota(jnp.int32, (used * slots, slots * PART), 0)
    source = lax.rem(line, slots) * PART + line // slots
    gather = jnp.where(
        source == lax.broadcasted_iota(jnp.int32, (used * slots, slots * PART), 1), 1.0, 0.0
    ).astype(BF16)
    inner_rows, outer_rows = [
        jnp.dot(
            gather, landing[part].reshape(slots * PART, LANES), preferred_element_type=F32
        )
        for part in range(2)
    ]
    lines = []
    for d in range(directions):
        for rows_of, turn in ((outer_rows, 0), (inner_rows, 0), (inner_rows, 1), (outer_rows, 1)):
            k = (2 * d + turn) * slots
            lines.append(rows_of[k : k + slots])
    whole = jnp.concatenate(lines, axis=1)
    for s in range(n):
        out_ref[s] = whole[SEND_CAP * s : SEND_CAP * s + SEND_CAP].astype(BF16)


def on_device(features, w_first, w_second, w_lift, w_merge, w_affine, tissue, owners):
    n = lax.axis_size("gz")
    channels, depth, ny, nx = features.shape
    cells = ny * nx
    hcells = (ny // 2) * nx
    flat = features.reshape(channels * depth, ny, nx)
    operands = (flat, w_first, w_second, w_lift, w_merge, w_affine, tissue, owners)
    per = SEND_CAP * PART
    blocks = (ny // BY) * (nx // BX)
    vmem = pl.BlockSpec(memory_space=pltpu.VMEM)
    routed = pl.pallas_call(
        functools.partial(kernel, n, ny),
        out_shape=jax.ShapeDtypeStruct((n, SEND_CAP, w_affine.shape[0] * depth * LANES), BF16),
        in_specs=[vmem] * len(operands),
        out_specs=vmem,
        scratch_shapes=[
            pltpu.VMEM((channels * depth * ny, LANES), F32),
            pltpu.VMEM((32, cells), BF16),
            pltpu.VMEM((576, 240), BF16),
            pltpu.VMEM((2, 192, LANES), F32),
            pltpu.VMEM((2, 216, LANES), F32),
            pltpu.VMEM((2, n, per, LANES), BF16),
            pltpu.VMEM((32, cells), BF16),
            pltpu.VMEM((240, cells + 2 * LANES), BF16),
            pltpu.VMEM((192, cells), BF16),
            pltpu.VMEM((96, hcells), BF16),
            pltpu.VMEM((576, hcells // 2), BF16),
            pltpu.VMEM((576, hcells // 2 + 2 * LANES), F32),
            pltpu.VMEM((192, cells + 2 * LANES), BF16),
            pltpu.VMEM((72, cells), F32),
            pltpu.VMEM((32, cells), BF16),
            pltpu.VMEM((32, cells), BF16),
            pltpu.VMEM((576, 576), BF16),
            pltpu.VMEM((648, 192), BF16),
            pltpu.VMEM((n * per, blocks * PART), BF16),
            pltpu.VMEM((blocks * PART, BY * LANES), BF16),
            pltpu.VMEM((2, blocks * PART, LANES), BF16),
            pltpu.VMEM((2, n * per, LANES), BF16),
            pltpu.SemaphoreType.DMA((2, 1)),
            pltpu.SemaphoreType.DMA((2, 1)),
            pltpu.SemaphoreType.DMA((2, SEGS)),
            pltpu.SemaphoreType.DMA((2, SEGS)),
            pltpu.SemaphoreType.DMA((2, ny // BY)),
            pltpu.SemaphoreType.DMA((2, ny // BY)),
            pltpu.SemaphoreType.DMA((2, n)),
            pltpu.SemaphoreType.DMA((2, n)),
        ],
        compiler_params=pltpu.CompilerParams(
            collective_id=0, has_side_effects=True, vmem_limit_bytes=48 * 1024 * 1024
        ),
        cost_estimate=pl.CostEstimate(
            flops=1600000000, bytes_accessed=2000000, transcendentals=65536
        ),
    )(*operands)
    return routed[None]


def solution(mesh):
    placed = (
        P(None, ("grp", "gz"), None, None),
        P(),
        P(),
        P(),
        P(),
        P(),
        P(("grp", "gz"), None),
        P(("grp", "gz"), None),
    )
    return jax.shard_map(
        on_device,
        mesh=mesh,
        in_specs=placed,
        out_specs=P(("grp", "gz"), None, None, None),
        check_vma=False,
    )
```
